512 devices in a mesh: dp: 8 (over x, core), ctx: 16 (over z), tp: 4 (over y).
Axes of the slice: x: 4, y: 4, z: 16, core: 2. Of those that a mesh axis runs over, the one named last changes fastest.
Arguments:
- tokens: bfloat16 [2048, 4096], P('ctx', ('dp', 'tp')), may hold values from -6 to 6
- expert_ids: int32 [2048, 8], P(('ctx', 'tp')), may hold values from 0 to 63, all different within a row; in each aligned block of 32 rows (0 to 31, 32 to 63, ...) at most 6 rows name the same one
- gate_codes: int32 [2048, 8], P(('ctx', 'tp')), may hold values from 16 to 255
- gate_weight: bfloat16 [64, 4096, 768], P(('ctx', 'tp'), 'dp'), may hold values from -0.09375 to 0.09375
- up_weight: bfloat16 [64, 4096, 768], P(('ctx', 'tp'), 'dp'), may hold values from -0.09375 to 0.09375
- down_weight: bfloat16 [64, 4096, 768], P(('ctx', 'tp'), 'dp'), may hold values from -0.21875 to 0.21875
- out_grad: bfloat16 [2048, 4096], P('ctx', ('dp', 'tp')), may hold values from -1.5 to 1.5
Outputs:
- layer_out: bfloat16 [2048, 4096], P(('ctx', 'tp'), 'dp')
- token_grad: bfloat16 [2048, 4096], P(('ctx', 'tp'), 'dp')
- gate_grad: bfloat16 [64, 4096, 768], P(('ctx', 'tp'), 'dp')
- up_grad: bfloat16 [64, 4096, 768], P(('ctx', 'tp'), 'dp')
- down_grad: bfloat16 [64, 4096, 768], P(('ctx', 'tp'), 'dp')
The draws below stay inside these ranges and needn't reach their ends.
Inputs may be any that keep to these rules, and one draw needn't show every extreme that they name: `expert_ids`: each row names 8 different experts. In each aligned block of 32 rows (the rows of one device of ctx+tp) no expert is named by more than 6 rows, and in some block an expert is named by exactly 6.
All inputs are finite; a program needn't handle non-finite values.
Results may differ from the reference program's by a relative error of at most 0.0064.
Values may be sent and summed in bfloat16 or wider, within the bound.
A program may use at most 64 MiB of HBM per device.

```python
import math
import jax
import jax.numpy as jnp
import numpy as np
from jax import lax

D = 4096
HID = 768
TOP = 8
EXPERTS = 64
TOK_FOLD = 32
CAP = 6
TOKENS = 2048
N_CTX = 16
N_TP = 4


def touch_ends(array, own_key, low, high):
    place = [jax.random.randint(jax.random.fold_in(own_key, axis), (), 0, length) for axis, length in enumerate(array.shape)]
    main_axis = array.shape.index(max(array.shape))
    beside = place[:main_axis] + [(place[main_axis] + 1) % array.shape[main_axis]] + place[main_axis + 1:]
    return array.at[tuple(place)].set(low).at[tuple(beside)].set(high)


def steps_of(stream_key, extent, pieces, least, top_value):
    def one(dim, blocks):
        draws = jax.random.uniform(jax.random.fold_in(jax.random.fold_in(stream_key, 6), dim), (blocks,), jnp.float32, least / len(pieces), top_value / len(pieces))
        return jnp.repeat(jnp.exp(draws), extent[dim] // blocks).reshape((-1,) + (1,) * (len(extent) - dim - 1))

    loudness = one(*pieces[0])
    for cut in pieces[1:]:
        loudness = loudness * one(*cut)
    return loudness


def assign_block(stream_key, own, number, rows, number_of, top, bound, skew):
    sequence = jax.random.permutation(stream_key, number_of)
    packed, usual = portions_of(number_of, rows * top, bound, skew, True), portions_of(number_of, rows * top, bound, skew, False)
    places = jnp.arange(number_of)

    def named(sizes, turn):
        used = int((sizes > 0).sum())
        fixed = max(1, used // 4)
        shifted = fixed + (places - fixed + turn * (used - fixed)) % max(1, number_of - fixed)
        return jnp.zeros((number_of,), jnp.int32).at[sequence[jnp.where(places < fixed, places, shifted)]].set(jnp.asarray(sizes, jnp.int32))

    sizes = jnp.where(number % 4 == 0, named(packed, number // 4), named(usual, number - number // 4 - 1))
    mixed = jax.random.permutation(jax.random.fold_in(own, 3), number_of)
    donor, taker = mixed[0:number_of // 2 * 2:2], mixed[1:number_of // 2 * 2:2]
    room = jnp.minimum(sizes[donor] - 1, bound - sizes[taker]) // 2
    room = jnp.where((donor == sequence[0]) | (taker == sequence[0]) | (sizes[taker] == 0), 0, jnp.maximum(room, 0))
    shifted = jax.random.randint(jax.random.fold_in(own, 4), (number_of // 2,), 0, 1 << 20) % (room + 1)
    sizes = sizes.at[donor].add(-shifted).at[taker].add(shifted)
    items = jnp.searchsorted(jnp.cumsum(sizes), jnp.arange(rows * top), side="right").astype(jnp.int32)
    table = items.reshape(top, rows).T
    table = table[jax.random.permutation(jax.random.fold_in(own, 1), rows)]
    turn = jax.random.randint(jax.random.fold_in(own, 2), (rows, 1), 0, top)
    return jnp.take_along_axis(table, (jnp.arange(top)[None, :] + turn) % top, axis=1)


def portions_of(amount, total, most, skew, full):
    portions = [(1 << 20) // math.isqrt(grade ** skew) + 1 for grade in range(1, amount + 1)]
    largest = most if full else min(most, max(-(-total // amount), total * portions[0] // sum(portions)))
    least = 1 if total - largest >= amount - 1 else 0
    holding, surplus = [largest] + [least] * (amount - 1), total - largest - least * (amount - 1)
    while surplus > 0:
        movable = [i for i in range(1, amount) if holding[i] < largest] or [i for i in range(1, amount) if holding[i] < most]
        mass, budget = sum([portions[i] for i in movable]), surplus
        for i in movable:
            addition = min(most - holding[i], max(1, budget * portions[i] // mass), surplus)
            holding[i] = holding[i] + addition
            surplus = surplus - addition
    return np.array(holding)


def gaussian(own_key, extent, scale, bound, split=(), kind=jnp.bfloat16):
    entries = jax.random.normal(own_key, extent, jnp.float32) * scale
    if len(split) > 0:
        entries = steps_of(own_key, extent, split, -0.22, 0.18) * entries
    return jnp.clip(entries, min=-bound, max=bound).astype(kind)


def setup_inputs(seed: int = 0) -> dict:
    key_list = jax.random.split(jax.random.key(seed), 8)
    tokens = gaussian(key_list[0], (TOKENS, D), 1.0, 6.0, ((0, 16), (1, 32)))
    expert_ids_keys = jax.random.split(jax.random.fold_in(key_list[1], 1), TOKENS // TOK_FOLD)
    expert_ids_turns = jax.random.permutation(jax.random.fold_in(key_list[1], 3), TOKENS // TOK_FOLD)
    expert_ids = jax.vmap(lambda own, number: assign_block(jax.random.fold_in(key_list[1], 2), own, number, TOK_FOLD, EXPERTS, TOP, CAP, 1))(expert_ids_keys, expert_ids_turns).reshape((TOKENS, TOP))
    gate_codes = touch_ends(jax.random.randint(key_list[2], (TOKENS, TOP), 16, 256), jax.random.fold_in(key_list[2], 1), 16, 255).astype(jnp.int32)
    gate_weight = gaussian(key_list[3], (EXPERTS, D, HID), D ** -0.5, 0.09375, ((0, 64), (1, 8)))
    up_weight = gaussian(key_list[4], (EXPERTS, D, HID), D ** -0.5, 0.09375, ((0, 64), (1, 8)))
    down_weight = gaussian(key_list[5], (EXPERTS, D, HID), HID ** -0.5, 0.21875, ((0, 64), (1, 8)))
    out_grad = gaussian(key_list[6], (TOKENS, D), 0.25, 1.5, ((0, 16), (1, 32)))
    return dict(tokens=tokens, expert_ids=expert_ids, gate_codes=gate_codes, gate_weight=gate_weight, up_weight=up_weight, down_weight=down_weight, out_grad=out_grad)


def reference(tokens, expert_ids, gate_codes, gate_weight, up_weight, down_weight, out_grad):
    count_all = TOKENS * TOP
    rows_most = N_CTX * N_TP * CAP
    flat_ids = expert_ids.reshape(-1).astype(jnp.int32)
    owners = (flat_ids[:, None] == jnp.arange(EXPERTS, dtype=jnp.int32)[None, :]).astype(jnp.int32)
    slot_index = jnp.sum((jnp.cumsum(owners, axis=0) - 1) * owners, axis=1).astype(jnp.int32)
    slot_table = jnp.full((EXPERTS, rows_most), count_all, jnp.int32)
    slot_table = slot_table.at[flat_ids, slot_index].set(jnp.arange(count_all, dtype=jnp.int32))
    token_pad = jnp.concatenate([tokens, jnp.zeros((1, D), jnp.bfloat16)], axis=0)
    grad_pad = jnp.concatenate([out_grad, jnp.zeros((1, D), jnp.bfloat16)], axis=0)
    weight_pad = jnp.concatenate([gate_codes.reshape(-1).astype(jnp.float32) / 256.0, jnp.zeros((1,), jnp.float32)])

    def expert_step(totals, inputs):
        mixed_sum, grad_sum = totals
        assigned, gate_w, up_w, down_w = inputs
        token_rows = (assigned // TOP).astype(jnp.int32)
        fold_rows = token_pad[token_rows]
        fold_grads = grad_pad[token_rows]
        weight = weight_pad[assigned]
        pre_gate = jnp.dot(fold_rows, gate_w, preferred_element_type=jnp.float32)
        pre_up = jnp.dot(fold_rows, up_w, preferred_element_type=jnp.float32)
        squash = jax.nn.sigmoid(pre_gate)
        hidden = (pre_gate * squash * pre_up).astype(jnp.bfloat16)
        expert_out = jnp.dot(hidden, down_w.T, preferred_element_type=jnp.float32).astype(jnp.bfloat16)
        slot_grad = (weight[:, None] * fold_grads.astype(jnp.float32)).astype(jnp.bfloat16)
        hidden_grad = jnp.dot(slot_grad, down_w, preferred_element_type=jnp.float32)
        gate_pre = (hidden_grad * pre_up * squash * (1.0 + pre_gate * (1.0 - squash))).astype(jnp.bfloat16)
        up_pre = (hidden_grad * pre_gate * squash).astype(jnp.bfloat16)
        row_grad = (jnp.dot(gate_pre, gate_w.T, preferred_element_type=jnp.float32)
                    + jnp.dot(up_pre, up_w.T, preferred_element_type=jnp.float32)).astype(jnp.bfloat16)
        mixed_sum = mixed_sum.at[token_rows].add(weight[:, None] * expert_out.astype(jnp.float32))
        grad_sum = grad_sum.at[token_rows].add(row_grad.astype(jnp.float32))
        gate_part = jnp.dot(fold_rows.T, gate_pre, preferred_element_type=jnp.float32).astype(jnp.bfloat16)
        up_part = jnp.dot(fold_rows.T, up_pre, preferred_element_type=jnp.float32).astype(jnp.bfloat16)
        down_part = jnp.dot(slot_grad.T, hidden, preferred_element_type=jnp.float32).astype(jnp.bfloat16)
        return (mixed_sum, grad_sum), (gate_part, up_part, down_part)

    start = (jnp.zeros((TOKENS + 1, D), jnp.float32), jnp.zeros((TOKENS + 1, D), jnp.float32))
    totals, parts = lax.scan(expert_step, start, (slot_table, gate_weight, up_weight, down_weight))
    layer_out = totals[0][:TOKENS].astype(jnp.bfloat16)
    token_grad = totals[1][:TOKENS].astype(jnp.bfloat16)
    return layer_out, token_grad, parts[0], parts[1], parts[2]
```

```python
import functools

import jax
import jax.numpy as jnp
from jax import lax
from jax.experimental import pallas as pl
from jax.experimental.pallas import tpu as pltpu
from jax.sharding import PartitionSpec as P

MESH = pl.DeviceIdType.MESH
F32 = jnp.float32
BF16 = jnp.bfloat16

NZ = 16
NY = 4
NX = 4
CAP = 6
BLOCK = 128
FOLD = 32
FEAT = 128
WIDE = 512
HID = 768
HALF = 384
ROWS = 192
PIECE = 48
OWN = 4
RING = (0, 1)


def mod(a, n):
    return lax.rem(a + 2 * n, n)


def nt(a, b):
    return lax.dot_general(a, b, (((1,), (1,)), ((), ())), preferred_element_type=F32)


def tn(a, b):
    return lax.dot_general(a, b, (((0,), (0,)), ((), ())), preferred_element_type=F32)


def nn(a, b):
    return jnp.dot(a, b, preferred_element_type=F32)


def body(
    ids_ref, codes_ref, tok_ref, grd_ref, wg_hbm, wu_hbm, wd_hbm,
    lo_ref, tg_ref, gg_hbm, ug_hbm, dg_hbm,
    data, meta_in, meta, wts, code_s, rank_s, gate_s, pick, pickg, ysend, rows_in,
    xs, core_out, core_in, part, opp_out, opp_in, back_out, back_in, fwd_out, fwd_in,
    act, full, ret_out, ret_in, cmat, acc, rs_out, rs_in, wgrad,
    z_send, z_recv, my_send, my_recv, y_send, y_recv, c_send, c_recv,
    x_send, x_recv, g_send, g_recv, r_send, r_recv, s_send, s_recv, l_sem, w_sem, o_sem,
):
    dp = lax.axis_index("dp")
    z = lax.axis_index("ctx")
    y = lax.axis_index("tp")
    x = dp // 2
    core = dp - 2 * x
    z_nb = (mod(z + 1, NZ), mod(z - 1, NZ))
    x_right = mod(x + 1, NX)
    x_left = mod(x - 1, NX)
    x_opp = mod(x + 2, NX)
    peer = {"dp": 2 * x + 1 - core}

    barrier = pltpu.get_barrier_semaphore()
    for nb in z_nb:
        pl.semaphore_signal(barrier, inc=1, device_id={"ctx": nb}, device_id_type=MESH)
    for dy in range(1, NY):
        pl.semaphore_signal(barrier, inc=1, device_id={"tp": mod(y + dy, NY)}, device_id_type=MESH)
    for xn in (x_right, x_left):
        pl.semaphore_signal(barrier, inc=1, device_id={"dp": 2 * xn + core}, device_id_type=MESH)
    pl.semaphore_signal(barrier, inc=1, device_id=peer, device_id_type=MESH)

    own_copies = [
        pltpu.make_async_copy(tok_ref, data.at[0, OWN], l_sem.at[0]),
        pltpu.make_async_copy(grd_ref, data.at[1, OWN], l_sem.at[1]),
    ]
    w_copies = [
        pltpu.make_async_copy(w.at[0], wts.at[i], w_sem.at[i])
        for i, w in enumerate((wg_hbm, wu_hbm, wd_hbm))
    ]
    for cp in own_copies + w_copies:
        cp.start()
    small = jnp.concatenate([ids_ref[...].astype(F32), codes_ref[...].astype(F32)], axis=0)
    place = (
        lax.broadcasted_iota(jnp.int32, (FOLD, BLOCK), 1)
        == y * FOLD + lax.broadcasted_iota(jnp.int32, (FOLD, BLOCK), 0)
    )
    place = jnp.where(place, 1.0, 0.0).astype(BF16)
    meta_in[0] = nn(small.astype(BF16), place).astype(BF16)

    pl.semaphore_wait(barrier, 8)

    def zcopy(stream, way, s):
        if way == 0:
            src, dst = mod(OWN - s + 1, NZ), mod(OWN - s, NZ)
        else:
            src, dst = OWN + s - 1, OWN + s
        buf = meta if stream == 2 else data.at[stream]
        return pltpu.make_async_remote_copy(
            src_ref=buf.at[src], dst_ref=buf.at[dst],
            send_sem=z_send.at[stream, way, s - 1], recv_sem=z_recv.at[stream, way, s - 1],
            device_id={"ctx": z_nb[way]}, device_id_type=MESH,
        )

    def zfirst(stream, way):
        src = (tok_ref, grd_ref)[stream]
        dst = OWN - 1 if way == 0 else OWN + 1
        return pltpu.make_async_remote_copy(
            src_ref=src, dst_ref=data.at[stream, dst],
            send_sem=z_send.at[stream, way, 0], recv_sem=z_recv.at[stream, way, 0],
            device_id={"ctx": z_nb[way]}, device_id_type=MESH,
        )

    def my_copy(dy):
        return pltpu.make_async_remote_copy(
            src_ref=meta_in.at[0], dst_ref=meta_in.at[dy],
            send_sem=my_send.at[dy - 1], recv_sem=my_recv.at[dy - 1],
            device_id={"tp": mod(y + dy, NY)}, device_id_type=MESH,
        )

    for dy in range(1, NY):
        my_copy(dy).start()
    for stream in (0, 1):
        for way in RING:
            zfirst(stream, way).start()
    for dy in range(1, NY):
        my_copy(dy).wait_recv()
    total = meta_in[0].astype(F32)
    for dy in range(1, NY):
        total = total + meta_in[dy].astype(F32)
    meta[OWN] = total.astype(BF16)
    for way in RING:
        zcopy(2, way, 1).start()

    longs = ((2, 0), (0, 0), (1, 1))
    shorts = ((2, 1), (0, 1), (1, 0))

    def zstep(s):
        for pair in longs + shorts:
            zcopy(*pair, s - 1).wait_recv()
            zcopy(*pair, s).start()

    def z_loop(first, last):
        def one(s, carry):
            zstep(s)
            return carry
        lax.fori_loop(first, last + 1, one, 0)

    lane = lax.broadcasted_iota(jnp.int32, (32, BLOCK), 1)
    row = lax.broadcasted_iota(jnp.int32, (32, BLOCK), 0)

    def route(c):
        block = meta[8 * c:8 * c + 8].astype(F32)
        ids, gts = block[:, :8], block[:, 8:] * (1.0 / 256.0)
        ms, gs = [], []
        for dy in range(NY):
            e = (NY * z + mod(y + dy, NY)).astype(F32)
            hit = ids == e
            ms.append(jnp.sum(jnp.where(hit, 1.0, 0.0), axis=1))
            gs.append(jnp.sum(jnp.where(hit, gts, 0.0), axis=1))
        m = jnp.concatenate(ms, axis=0)
        g = jnp.concatenate(gs, axis=0)
        a = lax.broadcasted_iota(jnp.int32, (BLOCK, BLOCK), 0)
        b = lax.broadcasted_iota(jnp.int32, (BLOCK, BLOCK), 1)
        tri = jnp.where((a < b) & (a // FOLD == b // FOLD), 1.0, 0.0).astype(BF16)
        rank = nn(m.astype(BF16), tri)
        base = (lane // FOLD) * PIECE + (row % 8) * CAP
        code_s[c] = jnp.where(m > 0.5, base.astype(F32) + rank, -1.0)
        rank_s[c] = jnp.where(m > 0.5, rank + 1.0, 0.0)
        gate_s[c] = g

    def pickers(c):
        slot = lax.broadcasted_iota(jnp.int32, (ROWS, BLOCK), 0).astype(F32)

        def one(i, carry):
            hit = slot == code_s[c, pl.ds(i, 1), :]
            at = (
                c,
                pl.ds(pl.multiple_of((i // 8) * ROWS, ROWS), ROWS),
                pl.ds(pl.multiple_of((i % 8) * BLOCK, BLOCK), BLOCK),
            )
            pick[at] = jnp.where(hit, 1.0, 0.0).astype(BF16)
            pickg[at] = jnp.where(hit, gate_s[c, pl.ds(i, 1), :], 0.0).astype(BF16)
            return carry
        lax.fori_loop(0, 32, one, 0)

    def ycopy(c, dy):
        return pltpu.make_async_remote_copy(
            src_ref=ysend.at[c, dy], dst_ref=rows_in.at[c, y],
            send_sem=y_send.at[c, dy - 1], recv_sem=y_recv.at[c, dy - 1],
            device_id={"tp": mod(y + dy, NY)}, device_id_type=MESH,
        )

    def select(c):
        tok = data[0, 8 * c:8 * c + 8].reshape(8 * BLOCK, FEAT)
        grd = data[1, 8 * c:8 * c + 8].reshape(8 * BLOCK, FEAT)
        for dy in (2, 1, 3, 0):
            r0 = nn(pick[c, dy * ROWS:(dy + 1) * ROWS, :], tok).astype(BF16)
            r1 = nn(pickg[c, dy * ROWS:(dy + 1) * ROWS, :], grd).astype(BF16)
            if dy == 0:
                rows_in[c, y, 0] = r0
                rows_in[c, y, 1] = r1
            else:
                ysend[c, dy, 0] = r0
                ysend[c, dy, 1] = r1
                ycopy(c, dy).start()

    def combiner(c):
        et = (
            lax.broadcasted_iota(jnp.int32, (FOLD, BLOCK), 1)
            == y * FOLD + lax.broadcasted_iota(jnp.int32, (FOLD, BLOCK), 0)
        )
        et = jnp.where(et, 1.0, 0.0).astype(BF16)
        rk = nt(et, rank_s[c].astype(BF16))
        gk = nt(et, gate_s[c].astype(BF16))
        col = lax.broadcasted_iota(jnp.int32, (FOLD, 32), 1)
        base = ((col // 8) * PIECE + (col % 8) * CAP - 1).astype(F32)
        tgt = jnp.where(rk > 0.5, base + rk, -1.0)
        out_lane = lax.broadcasted_iota(jnp.int32, (FOLD, ROWS), 1).astype(F32)
        for pp in range(8):
            ones = jnp.zeros((FOLD, ROWS), F32)
            gated = jnp.zeros((FOLD, ROWS), F32)
            for q in range(NY):
                k = q * 8 + pp
                hit = out_lane == tgt[:, k:k + 1]
                ones = jnp.where(hit, 1.0, ones)
                gated = jnp.where(hit, gk[:, k:k + 1], gated)
            cmat[c, 0, pp * FOLD:(pp + 1) * FOLD, :] = gated.astype(BF16)
            cmat[c, 1, pp * FOLD:(pp + 1) * FOLD, :] = ones.astype(BF16)

    mine = pl.ds(pl.multiple_of(core * HALF, HALF), HALF)
    other = pl.ds(pl.multiple_of((1 - core) * HALF, HALF), HALF)

    def core_copy(c):
        return pltpu.make_async_remote_copy(
            src_ref=core_out.at[c], dst_ref=core_in.at[c],
            send_sem=c_send.at[c], recv_sem=c_recv.at[c],
            device_id=peer, device_id_type=MESH,
        )

    def partials(c):
        for dy in range(1, NY):
            ycopy(c, dy).wait_recv()
        for a in (0, 1):
            xs[a, c * ROWS:(c + 1) * ROWS, :] = jnp.concatenate(
                [rows_in[c, yy, a] for yy in range(NY)], axis=1
            )
        for k in range(3):
            lhs = xs[k // 2, c * ROWS:(c + 1) * ROWS, :]
            core_out[c, :, k * HALF:(k + 1) * HALF] = nn(lhs, wts[k, :, other]).astype(BF16)
        core_copy(c).start()
        for k in range(3):
            lhs = xs[k // 2, c * ROWS:(c + 1) * ROWS, :]
            part[c, :, k * HALF:(k + 1) * HALF] = nn(lhs, wts[k, :, mine])

    def x_ends(c):
        return (x_right, x_left) if c == 0 else (x_left, x_right)

    def xcopy(c, kind):
        ahead, behind = x_ends(c)
        src, dst = ((opp_out, opp_in), (back_out, back_in), (fwd_out, fwd_in))[kind]
        to = behind if kind == 1 else ahead
        return pltpu.make_async_remote_copy(
            src_ref=src.at[c], dst_ref=dst.at[c],
            send_sem=x_send.at[c, kind], recv_sem=x_recv.at[c, kind],
            device_id={"dp": 2 * to + core}, device_id_type=MESH,
        )

    def piece(c, xx):
        at = pl.ds(pl.multiple_of(xx * PIECE, PIECE), PIECE)
        return part[c, at, :] + core_in[c, at, :].astype(F32)

    def x_first(c):
        core_copy(c).wait_recv()
        ahead, behind = x_ends(c)
        opp_out[c] = piece(c, x_opp).astype(BF16)
        xcopy(c, 0).start()
        back_out[c] = piece(c, behind).astype(BF16)
        xcopy(c, 1).start()

    def x_second(c):
        ahead, behind = x_ends(c)
        xcopy(c, 0).wait_recv()
        fwd_out[c] = (piece(c, ahead) + opp_in[c].astype(F32)).astype(BF16)
        xcopy(c, 2).start()

    def gcopy(c, k):
        ahead, behind = x_ends(c)
        slot = (x, x, x, behind, behind, ahead, x_opp)[k]
        to = (
            {"dp": 2 * ahead + core}, {"dp": 2 * behind + core}, peer,
            {"dp": 2 * ahead + core}, peer, peer, peer,
        )[k]
        return pltpu.make_async_remote_copy(
            src_ref=act.at[c, core, slot], dst_ref=act.at[c, core, slot],
            send_sem=g_send.at[c, k], recv_sem=g_recv.at[c, k],
            device_id=to, device_id_type=MESH,
        )

    def x_third(c):
        xcopy(c, 1).wait_recv()
        own = piece(c, x) + back_in[c].astype(F32)
        xcopy(c, 2).wait_recv()
        own = own + fwd_in[c].astype(F32)
        pre_gate, pre_up, hid_grad = own[:, :HALF], own[:, HALF:2 * HALF], own[:, 2 * HALF:]
        squash = jax.nn.sigmoid(pre_gate)
        act[c, core, x, :, :HALF] = (pre_gate * squash * pre_up).astype(BF16)
        act[c, core, x, :, HALF:2 * HALF] = (
            hid_grad * pre_up * squash * (1.0 + pre_gate * (1.0 - squash))
        ).astype(BF16)
        act[c, core, x, :, 2 * HALF:] = (hid_grad * pre_gate * squash).astype(BF16)
        for k in (0, 1, 2):
            gcopy(c, k).start()

    def gather(c):
        gcopy(c, 0).wait_recv()
        gcopy(c, 3).start()
        gcopy(c, 4).start()
        gcopy(c, 1).wait_recv()
        gcopy(c, 5).start()

    def gather_end(c):
        gcopy(c, 3).wait_recv()
        gcopy(c, 6).start()
        for k in (2, 4, 5, 6):
            gcopy(c, k).wait_recv()

    def rcopy(c, dy):
        return pltpu.make_async_remote_copy(
            src_ref=ret_out.at[c, mod(y + dy, NY)], dst_ref=ret_in.at[c, NY - dy],
            send_sem=r_send.at[c, dy - 1], recv_sem=r_recv.at[c, dy - 1],
            device_id={"tp": mod(y + dy, NY)}, device_id_type=MESH,
        )

    def results(c):
        at = slice(c * ROWS, (c + 1) * ROWS)
        for k in range(3):
            for h in (0, 1):
                full[k, at, h * HALF:(h + 1) * HALF] = act[
                    c, h, :, :, k * HALF:(k + 1) * HALF
                ].reshape(ROWS, HALF)
        eo = nt(full[0, at, :], wts[2]).astype(BF16)
        ret_out[c, :, 0] = eo.reshape(NY, PIECE, WIDE)
        rg = (nt(full[1, at, :], wts[0]) + nt(full[2, at, :], wts[1])).astype(BF16)
        ret_out[c, :, 1] = rg.reshape(NY, PIECE, WIDE)
        for dy in (2, 1, 3):
            rcopy(c, dy).start()
        ret_in[c, 0] = ret_out[c, y]

    def combine(c):
        for dy in range(1, NY):
            rcopy(c, dy).wait_recv()
        for a in (0, 1):
            got = ret_in[c, :, a].reshape(ROWS, WIDE)
            acc[a, 256 * c:256 * c + 256, :] = nn(cmat[c, a], got)

    def weight_grad(k):
        lhs = xs[k // 2]
        rhs = full[(1, 2, 0)[k]]
        wgrad[k] = tn(lhs, rhs).astype(BF16)
        pltpu.make_async_copy(wgrad.at[k], (gg_hbm, ug_hbm, dg_hbm)[k].at[0], o_sem.at[k]).start()

    def scopy(a, way, t):
        return pltpu.make_async_remote_copy(
            src_ref=rs_out.at[a, way, t], dst_ref=rs_in.at[a, way, t],
            send_sem=s_send.at[a, way, t], recv_sem=s_recv.at[a, way, t],
            device_id={"ctx": z_nb[way]}, device_id_type=MESH,
        )

    def steps_of(a, way):
        return 8 if a == way else 7

    def term(a, way, t):
        k = steps_of(a, way) - t
        p = mod(OWN + k, NZ) if way == 0 else mod(OWN - k, NZ)
        return acc[a, pl.ds(pl.multiple_of(p * FOLD, FOLD), FOLD), :]

    def sstep(a, way, t):
        scopy(a, way, t - 1).wait_recv()
        rs_out[a, way, t] = (term(a, way, t) + rs_in[a, way, t - 1].astype(F32)).astype(BF16)
        scopy(a, way, t).start()

    z_loop(2, 5)
    for cp in own_copies:
        cp.wait()
    route(0)
    pickers(0)
    select(0)
    zstep(6)
    for cp in w_copies:
        cp.wait()
    partials(0)
    zstep(7)
    x_first(0)
    for pair in longs:
        zcopy(*pair, 7).wait_recv()
        zcopy(*pair, 8).start()
    x_second(0)
    combiner(0)
    for pair in shorts:
        zcopy(*pair, 7).wait_recv()
    zcopy(2, 0, 8).wait_recv()
    route(1)
    pickers(1)
    for pair in longs[1:]:
        zcopy(*pair, 8).wait_recv()
    select(1)
    x_third(0)
    combiner(1)
    partials(1)
    gather(0)
    x_first(1)
    gather_end(0)
    x_second(1)
    results(0)
    x_third(1)
    gather(1)
    combine(0)
    gather_end(1)
    results(1)
    weight_grad(0)
    weight_grad(1)
    weight_grad(2)
    combine(1)
    for a in (0, 1):
        for way in RING:
            rs_out[a, way, 0] = term(a, way, 0).astype(BF16)
            scopy(a, way, 0).start()

    def ring(t, carry):
        for a in (0, 1):
            for way in RING:
                sstep(a, way, t)
        return carry

    lax.fori_loop(1, 7, ring, 0)
    sstep(0, 0, 7)
    sstep(1, 1, 7)
    for a, ref in ((0, lo_ref), (1, tg_ref)):
        short = 1 - a
        scopy(a, short, 6).wait_recv()
        got = acc[a, OWN * FOLD:(OWN + 1) * FOLD, :] + rs_in[a, short, 6].astype(F32)
        scopy(a, a, 7).wait_recv()
        ref[...] = (got + rs_in[a, a, 7].astype(F32)).astype(BF16)

    for dy in range(1, NY):
        my_copy(dy).wait_send()
        for c in (0, 1):
            ycopy(c, dy).wait_send()
            rcopy(c, dy).wait_send()
    for pair in longs + shorts:
        def left(s, carry, pair=pair):
            zcopy(*pair, s).wait_send()
            return carry
        lax.fori_loop(2 if pair[0] < 2 else 1, 9 if pair in longs else 8, left, 0)
        if pair[0] < 2:
            zfirst(*pair).wait_send()
    for c in (0, 1):
        core_copy(c).wait_send()
        for kind in range(3):
            xcopy(c, kind).wait_send()
        for k in range(7):
            gcopy(c, k).wait_send()
    for a in (0, 1):
        for way in RING:
            def gone(t, carry, a=a, way=way):
                scopy(a, way, t).wait_send()
                return carry
            lax.fori_loop(0, steps_of(a, way), gone, 0)
    for k in range(3):
        pltpu.make_async_copy(
            wgrad.at[k], (gg_hbm, ug_hbm, dg_hbm)[k].at[0], o_sem.at[k]
        ).wait()


def shards(tokens, expert_ids, gate_codes, gate_weight, up_weight, down_weight, out_grad):
    vmem = pl.BlockSpec(memory_space=pltpu.VMEM)
    hbm = pl.BlockSpec(memory_space=pltpu.HBM)
    dma = pltpu.SemaphoreType.DMA
    wide3 = 3 * HALF
    scratch = [
        pltpu.VMEM((2, NZ, BLOCK, FEAT), BF16),
        pltpu.VMEM((NY, 16, BLOCK), BF16),
        pltpu.VMEM((NZ, 16, BLOCK), BF16),
        pltpu.VMEM((3, WIDE, HID), BF16),
        pltpu.VMEM((2, 32, BLOCK), F32),
        pltpu.VMEM((2, 32, BLOCK), F32),
        pltpu.VMEM((2, 32, BLOCK), F32),
        pltpu.VMEM((2, NY * ROWS, 8 * BLOCK), BF16),
        pltpu.VMEM((2, NY * ROWS, 8 * BLOCK), BF16),
        pltpu.VMEM((2, NY, 2, ROWS, FEAT), BF16),
        pltpu.VMEM((2, NY, 2, ROWS, FEAT), BF16),
        pltpu.VMEM((2, 2 * ROWS, WIDE), BF16),
        pltpu.VMEM((2, ROWS, wide3), BF16),
        pltpu.VMEM((2, ROWS, wide3), BF16),
        pltpu.VMEM((2, ROWS, wide3), F32),
    ] + [pltpu.VMEM((2, PIECE, wide3), BF16)] * 6 + [
        pltpu.VMEM((2, 2, NX, PIECE, wide3), BF16),
        pltpu.VMEM((3, 2 * ROWS, HID), BF16),
        pltpu.VMEM((2, NY, 2, PIECE, WIDE), BF16),
        pltpu.VMEM((2, NY, 2, PIECE, WIDE), BF16),
        pltpu.VMEM((2, 2, 8 * FOLD, ROWS), BF16),
        pltpu.VMEM((2, NZ * FOLD, WIDE), F32),
        pltpu.VMEM((2, 2, 8, FOLD, WIDE), BF16),
        pltpu.VMEM((2, 2, 8, FOLD, WIDE), BF16),
        pltpu.VMEM((3, WIDE, HID), BF16),
        dma((3, 2, 8)), dma((3, 2, 8)),
        dma((3,)), dma((3,)),
        dma((2, 3)), dma((2, 3)),
        dma((2,)), dma((2,)),
        dma((2, 3)), dma((2, 3)),
        dma((2, 7)), dma((2, 7)),
        dma((2, 3)), dma((2, 3)),
        dma((2, 2, 8)), dma((2, 2, 8)),
        dma((2,)), dma((3,)), dma((3,)),
    ]
    fold = jax.ShapeDtypeStruct((FOLD, WIDE), BF16)
    weight = jax.ShapeDtypeStruct((1, WIDE, HID), BF16)
    return pl.pallas_call(
        body,
        out_shape=(fold, fold, weight, weight, weight),
        in_specs=[vmem, vmem, hbm, hbm, hbm, hbm, hbm],
        out_specs=(vmem, vmem, hbm, hbm, hbm),
        scratch_shapes=scratch,
        compiler_params=pltpu.CompilerParams(
            collective_id=0, has_side_effects=True, vmem_limit_bytes=56 * 1024 * 1024
        ),
    )(
        expert_ids.T, gate_codes.T, tokens, out_grad, gate_weight, up_weight, down_weight
    )


def solution(mesh):
    placed = (
        P("ctx", ("dp", "tp")),
        P(("ctx", "tp"), None),
        P(("ctx", "tp"), None),
        P(("ctx", "tp"), "dp", None),
        P(("ctx", "tp"), "dp", None),
        P(("ctx", "tp"), "dp", None),
        P("ctx", ("dp", "tp")),
    )
    return jax.shard_map(
        shards,
        mesh=mesh,
        in_specs=placed,
        out_specs=(
            P(("ctx", "tp"), "dp"),
            P(("ctx", "tp"), "dp"),
            P(("ctx", "tp"), "dp", None),
            P(("ctx", "tp"), "dp", None),
            P(("ctx", "tp"), "dp", None),
        ),
        check_vma=False,
    )
```

```python
import functools

import jax
import jax.numpy as jnp
from jax import lax
from jax.experimental import pallas as pl
from jax.experimental.pallas import tpu as pltpu
from jax.sharding import PartitionSpec as P

MESH = pl.DeviceIdType.MESH
F32 = jnp.float32
BF16 = jnp.bfloat16

NZ = 16
NY = 4
NX = 4
CAP = 6
BLOCK = 128
FOLD = 32
FEAT = 128
WIDE = 512
HID = 768
HALF = 384
ROWS = 192
PIECE = 48
OWN = 4
RING = (0, 1)


def mod(a, n):
    return lax.rem(a + 2 * n, n)


def nt(a, b):
    return lax.dot_general(a, b, (((1,), (1,)), ((), ())), preferred_element_type=F32)


def tn(a, b):
    return lax.dot_general(a, b, (((0,), (0,)), ((), ())), preferred_element_type=F32)


def nn(a, b):
    return jnp.dot(a, b, preferred_element_type=F32)


def body(
    ids_ref, codes_ref, tok_ref, grd_ref, wg_hbm, wu_hbm, wd_hbm,
    lo_ref, tg_ref, gg_hbm, ug_hbm, dg_hbm,
    data, meta_in, meta, wts, code_s, rank_s, gate_s, pick, pickg, ysend, rows_in,
    xs, core_out, core_in, part, opp_out, opp_in, back_out, back_in, fwd_out, fwd_in,
    act, full, ret_out, ret_in, cmat, acc, rs_out, rs_in, wgrad,
    z_send, z_recv, my_send, my_recv, y_send, y_recv, c_send, c_recv,
    x_send, x_recv, g_send, g_recv, r_send, r_recv, s_send, s_recv, l_sem, w_sem, o_sem,
):
    dp = lax.axis_index("dp")
    z = lax.axis_index("ctx")
    y = lax.axis_index("tp")
    x = dp // 2
    core = dp - 2 * x
    z_nb = (mod(z + 1, NZ), mod(z - 1, NZ))
    z_nb2 = (mod(z + 2, NZ), mod(z - 2, NZ))
    x_right = mod(x + 1, NX)
    x_left = mod(x - 1, NX)
    x_opp = mod(x + 2, NX)
    peer = {"dp": 2 * x + 1 - core}

    barrier = pltpu.get_barrier_semaphore()
    for nb in z_nb + z_nb2:
        pl.semaphore_signal(barrier, inc=1, device_id={"ctx": nb}, device_id_type=MESH)
    for dy in range(1, NY):
        pl.semaphore_signal(barrier, inc=1, device_id={"tp": mod(y + dy, NY)}, device_id_type=MESH)
    for xn in (x_right, x_left):
        pl.semaphore_signal(barrier, inc=1, device_id={"dp": 2 * xn + core}, device_id_type=MESH)
    pl.semaphore_signal(barrier, inc=1, device_id=peer, device_id_type=MESH)

    own_copies = [
        pltpu.make_async_copy(tok_ref, data.at[0, OWN], l_sem.at[0]),
        pltpu.make_async_copy(grd_ref, data.at[1, OWN], l_sem.at[1]),
    ]
    w_copies = [
        pltpu.make_async_copy(w.at[0], wts.at[i], w_sem.at[i])
        for i, w in enumerate((wg_hbm, wu_hbm, wd_hbm))
    ]
    for cp in own_copies + w_copies:
        cp.start()
    small = jnp.concatenate([ids_ref[...].astype(F32), codes_ref[...].astype(F32)], axis=0)
    place = (
        lax.broadcasted_iota(jnp.int32, (FOLD, BLOCK), 1)
        == y * FOLD + lax.broadcasted_iota(jnp.int32, (FOLD, BLOCK), 0)
    )
    place = jnp.where(place, 1.0, 0.0).astype(BF16)
    meta_in[0] = nn(small.astype(BF16), place).astype(BF16)

    pl.semaphore_wait(barrier, 10)

    def at_distance(way, d):
        return (OWN - d) % NZ if way == 0 else (OWN + d) % NZ

    def zcopy(stream, way, d):
        hop = 2 if d % 2 == 0 else 1
        buf = meta if stream == 2 else data.at[stream]
        if d == hop and stream < 2:
            src = (tok_ref, grd_ref)[stream]
        else:
            src = buf.at[at_distance(way, d - hop)]
        return pltpu.make_async_remote_copy(
            src_ref=src, dst_ref=buf.at[at_distance(way, d)],
            send_sem=z_send.at[stream, way, d - 1], recv_sem=z_recv.at[stream, way, d - 1],
            device_id={"ctx": (z_nb, z_nb2)[hop - 1][way]}, device_id_type=MESH,
        )

    def reach(stream, way):
        return 8 if (stream == 1) == (way == 1) else 7

    def my_copy(dy):
        return pltpu.make_async_remote_copy(
            src_ref=meta_in.at[0], dst_ref=meta_in.at[dy],
            send_sem=my_send.at[dy - 1], recv_sem=my_recv.at[dy - 1],
            device_id={"tp": mod(y + dy, NY)}, device_id_type=MESH,
        )

    for dy in range(1, NY):
        my_copy(dy).start()
    values = ((0, 0), (1, 1), (0, 1), (1, 0))
    routes = ((2, 0), (2, 1))
    for pair in values:
        zcopy(*pair, 2).start()
    for pair in values:
        zcopy(*pair, 1).start()
    for dy in range(1, NY):
        my_copy(dy).wait_recv()
    total = meta_in[0].astype(F32)
    for dy in range(1, NY):
        total = total + meta_in[dy].astype(F32)
    meta[OWN] = total.astype(BF16)
    for pair in routes:
        zcopy(*pair, 2).start()
        zcopy(*pair, 1).start()

    def relay(d):
        for pair in routes + values:
            zcopy(*pair, d).wait_recv()
            if d + 2 <= reach(*pair):
                zcopy(*pair, d + 2).start()
        for pair in routes + values:
            zcopy(*pair, d + 1).start()

    def arrived(pairs, first, last):
        for pair in pairs:
            for d in range(first, min(last, reach(*pair)) + 1):
                if d % 2 == 1 or d == 8:
                    zcopy(*pair, d).wait_recv()

    lane = lax.broadcasted_iota(jnp.int32, (32, BLOCK), 1)
    row = lax.broadcasted_iota(jnp.int32, (32, BLOCK), 0)

    def route(c):
        block = meta[8 * c:8 * c + 8].astype(F32)
        ids, gts = block[:, :8], block[:, 8:] * (1.0 / 256.0)
        ms, gs = [], []
        for dy in range(NY):
            e = (NY * z + mod(y + dy, NY)).astype(F32)
            hit = ids == e
            ms.append(jnp.sum(jnp.where(hit, 1.0, 0.0), axis=1))
            gs.append(jnp.sum(jnp.where(hit, gts, 0.0), axis=1))
        m = jnp.concatenate(ms, axis=0)
        g = jnp.concatenate(gs, axis=0)
        a = lax.broadcasted_iota(jnp.int32, (BLOCK, BLOCK), 0)
        b = lax.broadcasted_iota(jnp.int32, (BLOCK, BLOCK), 1)
        tri = jnp.where((a < b) & (a // FOLD == b // FOLD), 1.0, 0.0).astype(BF16)
        rank = nn(m.astype(BF16), tri)
        base = (lane // FOLD) * PIECE + (row % 8) * CAP
        code_s[c] = jnp.where(m > 0.5, base.astype(F32) + rank, -1.0)
        rank_s[c] = jnp.where(m > 0.5, rank + 1.0, 0.0)
        gate_s[c] = g

    def pickers(c):
        slot = lax.broadcasted_iota(jnp.int32, (ROWS, BLOCK), 0).astype(F32)

        def one(i, carry):
            hit = slot == code_s[c, pl.ds(i, 1), :]
            at = (
                c,
                pl.ds(pl.multiple_of((i // 8) * ROWS, ROWS), ROWS),
                pl.ds(pl.multiple_of((i % 8) * BLOCK, BLOCK), BLOCK),
            )
            pick[at] = jnp.where(hit, 1.0, 0.0).astype(BF16)
            pickg[at] = jnp.where(hit, gate_s[c, pl.ds(i, 1), :], 0.0).astype(BF16)
            return carry
        lax.fori_loop(0, 32, one, 0)

    def ycopy(c, dy):
        return pltpu.make_async_remote_copy(
            src_ref=ysend.at[c, dy], dst_ref=rows_in.at[c, y],
            send_sem=y_send.at[c, dy - 1], recv_sem=y_recv.at[c, dy - 1],
            device_id={"tp": mod(y + dy, NY)}, device_id_type=MESH,
        )

    def select(c):
        tok = data[0, 8 * c:8 * c + 8].reshape(8 * BLOCK, FEAT)
        grd = data[1, 8 * c:8 * c + 8].reshape(8 * BLOCK, FEAT)
        for dy in (2, 1, 3, 0):
            r0 = nn(pick[c, dy * ROWS:(dy + 1) * ROWS, :], tok).astype(BF16)
            r1 = nn(pickg[c, dy * ROWS:(dy + 1) * ROWS, :], grd).astype(BF16)
            if dy == 0:
                rows_in[c, y, 0] = r0
                rows_in[c, y, 1] = r1
            else:
                ysend[c, dy, 0] = r0
                ysend[c, dy, 1] = r1
                ycopy(c, dy).start()

    def combiner(c):
        et = (
            lax.broadcasted_iota(jnp.int32, (FOLD, BLOCK), 1)
            == y * FOLD + lax.broadcasted_iota(jnp.int32, (FOLD, BLOCK), 0)
        )
        et = jnp.where(et, 1.0, 0.0).astype(BF16)
        rk = nt(et, rank_s[c].astype(BF16))
        gk = nt(et, gate_s[c].astype(BF16))
        col = lax.broadcasted_iota(jnp.int32, (FOLD, 32), 1)
        base = ((col // 8) * PIECE + (col % 8) * CAP - 1).astype(F32)
        tgt = jnp.where(rk > 0.5, base + rk, -1.0)
        out_lane = lax.broadcasted_iota(jnp.int32, (FOLD, ROWS), 1).astype(F32)
        for pp in range(8):
            ones = jnp.zeros((FOLD, ROWS), F32)
            gated = jnp.zeros((FOLD, ROWS), F32)
            for q in range(NY):
                k = q * 8 + pp
                hit = out_lane == tgt[:, k:k + 1]
                ones = jnp.where(hit, 1.0, ones)
                gated = jnp.where(hit, gk[:, k:k + 1], gated)
            cmat[c, 0, pp * FOLD:(pp + 1) * FOLD, :] = gated.astype(BF16)
            cmat[c, 1, pp * FOLD:(pp + 1) * FOLD, :] = ones.astype(BF16)

    mine = pl.ds(pl.multiple_of(core * HALF, HALF), HALF)
    other = pl.ds(pl.multiple_of((1 - core) * HALF, HALF), HALF)

    def core_copy(c, k):
        return pltpu.make_async_remote_copy(
            src_ref=core_out.at[c, k], dst_ref=core_in.at[c, k],
            send_sem=c_send.at[c, k], recv_sem=c_recv.at[c, k],
            device_id=peer, device_id_type=MESH,
        )

    def partials(c):
        for dy in range(1, NY):
            ycopy(c, dy).wait_recv()
        for a in (0, 1):
            xs[a, c * ROWS:(c + 1) * ROWS, :] = jnp.concatenate(
                [rows_in[c, yy, a] for yy in range(NY)], axis=1
            )
        for k in range(3):
            lhs = xs[k // 2, c * ROWS:(c + 1) * ROWS, :]
            core_out[c, k] = nn(lhs, wts[k, :, other]).astype(BF16)
            core_copy(c, k).start()
        for k in range(3):
            lhs = xs[k // 2, c * ROWS:(c + 1) * ROWS, :]
            part[c, k] = nn(lhs, wts[k, :, mine])

    def x_ends(c):
        return (x_right, x_left) if c == 0 else (x_left, x_right)

    def xcopy(c, kind, k):
        ahead, behind = x_ends(c)
        src, dst = ((opp_out, opp_in), (back_out, back_in), (fwd_out, fwd_in))[kind]
        to = behind if kind == 1 else ahead
        return pltpu.make_async_remote_copy(
            src_ref=src.at[c, k], dst_ref=dst.at[c, k],
            send_sem=x_send.at[c, kind, k], recv_sem=x_recv.at[c, kind, k],
            device_id={"dp": 2 * to + core}, device_id_type=MESH,
        )

    def piece(c, k, xx):
        at = pl.ds(pl.multiple_of(xx * PIECE, PIECE), PIECE)
        return part[c, k, at, :] + core_in[c, k, at, :].astype(F32)

    def x_first(c):
        ahead, behind = x_ends(c)
        for k in range(3):
            core_copy(c, k).wait_recv()
            opp_out[c, k] = piece(c, k, x_opp).astype(BF16)
            xcopy(c, 0, k).start()
            back_out[c, k] = piece(c, k, behind).astype(BF16)
            xcopy(c, 1, k).start()

    def x_second(c):
        ahead, behind = x_ends(c)
        for k in range(3):
            xcopy(c, 0, k).wait_recv()
            fwd_out[c, k] = (piece(c, k, ahead) + opp_in[c, k].astype(F32)).astype(BF16)
            xcopy(c, 2, k).start()

    def gcopy(c, k):
        ahead, behind = x_ends(c)
        slot = (x, x, x, behind, behind, ahead, x_opp)[k]
        to = (
            {"dp": 2 * ahead + core}, {"dp": 2 * behind + core}, peer,
            {"dp": 2 * ahead + core}, peer, peer, peer,
        )[k]
        return pltpu.make_async_remote_copy(
            src_ref=act.at[c, core, slot], dst_ref=act.at[c, core, slot],
            send_sem=g_send.at[c, k], recv_sem=g_recv.at[c, k],
            device_id=to, device_id_type=MESH,
        )

    def x_third(c):
        sums = []
        for k in range(3):
            xcopy(c, 1, k).wait_recv()
            xcopy(c, 2, k).wait_recv()
            sums.append(
                piece(c, k, x) + back_in[c, k].astype(F32) + fwd_in[c, k].astype(F32)
            )
        pre_gate, pre_up, hid_grad = sums
        squash = jax.nn.sigmoid(pre_gate)
        act[c, core, x, :, :HALF] = (pre_gate * squash * pre_up).astype(BF16)
        act[c, core, x, :, HALF:2 * HALF] = (
            hid_grad * pre_up * squash * (1.0 + pre_gate * (1.0 - squash))
        ).astype(BF16)
        act[c, core, x, :, 2 * HALF:] = (hid_grad * pre_gate * squash).astype(BF16)
        for k in (0, 1, 2):
            gcopy(c, k).start()

    def gather(c):
        gcopy(c, 0).wait_recv()
        gcopy(c, 3).start()
        gcopy(c, 4).start()
        gcopy(c, 1).wait_recv()
        gcopy(c, 5).start()

    def gather_end(c):
        gcopy(c, 3).wait_recv()
        gcopy(c, 6).start()
        for k in (2, 4, 5, 6):
            gcopy(c, k).wait_recv()

    def rcopy(c, dy):
        return pltpu.make_async_remote_copy(
            src_ref=ret_out.at[c, mod(y + dy, NY)], dst_ref=ret_in.at[c, NY - dy],
            send_sem=r_send.at[c, dy - 1], recv_sem=r_recv.at[c, dy - 1],
            device_id={"tp": mod(y + dy, NY)}, device_id_type=MESH,
        )

    def results(c):
        at = slice(c * ROWS, (c + 1) * ROWS)
        for k in range(3):
            for h in (0, 1):
                full[k, at, h * HALF:(h + 1) * HALF] = act[
                    c, h, :, :, k * HALF:(k + 1) * HALF
                ].reshape(ROWS, HALF)
        eo = nt(full[0, at, :], wts[2]).astype(BF16)
        ret_out[c, :, 0] = eo.reshape(NY, PIECE, WIDE)
        rg = (nt(full[1, at, :], wts[0]) + nt(full[2, at, :], wts[1])).astype(BF16)
        ret_out[c, :, 1] = rg.reshape(NY, PIECE, WIDE)
        for dy in (2, 1, 3):
            rcopy(c, dy).start()
        ret_in[c, 0] = ret_out[c, y]

    def combine(c):
        for dy in range(1, NY):
            rcopy(c, dy).wait_recv()
        for a in (0, 1):
            got = ret_in[c, :, a].reshape(ROWS, WIDE)
            acc[a, 256 * c:256 * c + 256, :] = nn(cmat[c, a], got)

    def weight_grad(k):
        lhs = xs[k // 2]
        rhs = full[(1, 2, 0)[k]]
        wgrad[k] = tn(lhs, rhs).astype(BF16)
        pltpu.make_async_copy(wgrad.at[k], (gg_hbm, ug_hbm, dg_hbm)[k].at[0], o_sem.at[k]).start()

    def scopy(a, way, d):
        hop = 2 if d % 2 == 0 else 1
        return pltpu.make_async_remote_copy(
            src_ref=rs_out.at[a, way, d - 1], dst_ref=rs_in.at[a, way, d - 1],
            send_sem=s_send.at[a, way, d - 1], recv_sem=s_recv.at[a, way, d - 1],
            device_id={"ctx": (z_nb, z_nb2)[hop - 1][way]}, device_id_type=MESH,
        )

    def span(a, way):
        return 8 if a == way else 7

    def collected(a, way, d):
        p = (OWN + d) % NZ if way == 0 else (OWN - d) % NZ
        value = acc[a, p * FOLD:(p + 1) * FOLD, :]
        if d % 2 == 0:
            for e in (d + 1, d + 2):
                if e <= span(a, way):
                    scopy(a, way, e).wait_recv()
                    value = value + rs_in[a, way, e - 1].astype(F32)
        return value

    flows = ((0, 0), (1, 1), (0, 1), (1, 0))

    def send_sums(d):
        for a, way in flows:
            if d <= span(a, way):
                rs_out[a, way, d - 1] = collected(a, way, d).astype(BF16)
                scopy(a, way, d).start()

    relay(2)
    relay(4)
    arrived(routes, 1, 4)
    route(0)
    pickers(0)
    relay(6)
    for cp in own_copies:
        cp.wait()
    arrived(values, 1, 4)
    select(0)
    arrived(routes, 5, 8)
    route(1)
    pickers(1)
    arrived(values, 5, 8)
    select(1)
    for cp in w_copies:
        cp.wait()
    partials(0)
    combiner(0)
    x_first(0)
    partials(1)
    x_second(0)
    x_first(1)
    combiner(1)
    x_third(0)
    x_second(1)
    gather(0)
    x_third(1)
    gather_end(0)
    results(0)
    gather(1)
    gather_end(1)
    results(1)
    weight_grad(0)
    combine(0)
    weight_grad(1)
    weight_grad(2)
    combine(1)
    send_sums(8)
    send_sums(7)
    for d in (6, 5, 4, 3, 2, 1):
        send_sums(d)
    for a, ref in ((0, lo_ref), (1, tg_ref)):
        value = acc[a, OWN * FOLD:(OWN + 1) * FOLD, :]
        for way in RING:
            for d in (1, 2):
                scopy(a, way, d).wait_recv()
                value = value + rs_in[a, way, d - 1].astype(F32)
        ref[...] = value.astype(BF16)

    for dy in range(1, NY):
        my_copy(dy).wait_send()
        for c in (0, 1):
            ycopy(c, dy).wait_send()
            rcopy(c, dy).wait_send()
    for pair in routes + values:
        for d in range(1, reach(*pair) + 1):
            zcopy(*pair, d).wait_send()
    for c in (0, 1):
        for k in range(3):
            core_copy(c, k).wait_send()
            for kind in range(3):
                xcopy(c, kind, k).wait_send()
        for k in range(7):
            gcopy(c, k).wait_send()
    for a, way in flows:
        for d in range(1, span(a, way) + 1):
            scopy(a, way, d).wait_send()
    for k in range(3):
        pltpu.make_async_copy(
            wgrad.at[k], (gg_hbm, ug_hbm, dg_hbm)[k].at[0], o_sem.at[k]
        ).wait()


def keep_body(*refs):
    sources, results, held, sems = refs[:5], refs[5:10], refs[10:15], refs[15]
    into = [pltpu.make_async_copy(sources[i], held[i], sems.at[0, i]) for i in range(5)]
    out = [pltpu.make_async_copy(held[i], results[i], sems.at[1, i]) for i in range(5)]
    for cp in into:
        cp.start()
    for first, second in zip(into, out):
        first.wait()
        second.start()
    for cp in out:
        cp.wait()


def shards(tokens, expert_ids, gate_codes, gate_weight, up_weight, down_weight, out_grad):
    vmem = pl.BlockSpec(memory_space=pltpu.VMEM)
    hbm = pl.BlockSpec(memory_space=pltpu.HBM)
    dma = pltpu.SemaphoreType.DMA
    wide3 = 3 * HALF
    scratch = [
        pltpu.VMEM((2, NZ, BLOCK, FEAT), BF16),
        pltpu.VMEM((NY, 16, BLOCK), BF16),
        pltpu.VMEM((NZ, 16, BLOCK), BF16),
        pltpu.VMEM((3, WIDE, HID), BF16),
        pltpu.VMEM((2, 32, BLOCK), F32),
        pltpu.VMEM((2, 32, BLOCK), F32),
        pltpu.VMEM((2, 32, BLOCK), F32),
        pltpu.VMEM((2, NY * ROWS, 8 * BLOCK), BF16),
        pltpu.VMEM((2, NY * ROWS, 8 * BLOCK), BF16),
        pltpu.VMEM((2, NY, 2, ROWS, FEAT), BF16),
        pltpu.VMEM((2, NY, 2, ROWS, FEAT), BF16),
        pltpu.VMEM((2, 2 * ROWS, WIDE), BF16),
        pltpu.VMEM((2, 3, ROWS, HALF), BF16),
        pltpu.VMEM((2, 3, ROWS, HALF), BF16),
        pltpu.VMEM((2, 3, ROWS, HALF), F32),
    ] + [pltpu.VMEM((2, 3, PIECE, HALF), BF16)] * 6 + [
        pltpu.VMEM((2, 2, NX, PIECE, wide3), BF16),
        pltpu.VMEM((3, 2 * ROWS, HID), BF16),
        pltpu.VMEM((2, NY, 2, PIECE, WIDE), BF16),
        pltpu.VMEM((2, NY, 2, PIECE, WIDE), BF16),
        pltpu.VMEM((2, 2, 8 * FOLD, ROWS), BF16),
        pltpu.VMEM((2, NZ * FOLD, WIDE), F32),
        pltpu.VMEM((2, 2, 8, FOLD, WIDE), BF16),
        pltpu.VMEM((2, 2, 8, FOLD, WIDE), BF16),
        pltpu.VMEM((3, WIDE, HID), BF16),
        dma((3, 2, 8)), dma((3, 2, 8)),
        dma((3,)), dma((3,)),
        dma((2, 3)), dma((2, 3)),
        dma((2, 3)), dma((2, 3)),
        dma((2, 3, 3)), dma((2, 3, 3)),
        dma((2, 7)), dma((2, 7)),
        dma((2, 3)), dma((2, 3)),
        dma((2, 2, 8)), dma((2, 2, 8)),
        dma((2,)), dma((3,)), dma((3,)),
    ]
    fold = jax.ShapeDtypeStruct((FOLD, WIDE), BF16)
    weight = jax.ShapeDtypeStruct((1, WIDE, HID), BF16)
    hbm5 = (hbm,) * 5
    results = pl.pallas_call(
        body,
        out_shape=(fold, fold, weight, weight, weight),
        in_specs=[vmem, vmem, hbm, hbm, hbm, hbm, hbm],
        out_specs=(vmem, vmem, hbm, hbm, hbm),
        scratch_shapes=scratch,
        compiler_params=pltpu.CompilerParams(
            collective_id=0, has_side_effects=True, vmem_limit_bytes=56 * 1024 * 1024
        ),
    )(
        expert_ids.T, gate_codes.T, tokens, out_grad, gate_weight, up_weight, down_weight
    )
    return pl.pallas_call(
        keep_body,
        out_shape=(fold, fold, weight, weight, weight),
        in_specs=hbm5,
        out_specs=hbm5,
        scratch_shapes=[pltpu.VMEM(out.shape, BF16) for out in (fold, fold, weight, weight, weight)]
        + [dma((2, 5))],
    )(*results)


def solution(mesh):
    placed = (
        P("ctx", ("dp", "tp")),
        P(("ctx", "tp"), None),
        P(("ctx", "tp"), None),
        P(("ctx", "tp"), "dp", None),
        P(("ctx", "tp"), "dp", None),
        P(("ctx", "tp"), "dp", None),
        P("ctx", ("dp", "tp")),
    )
    return jax.shard_map(
        shards,
        mesh=mesh,
        in_specs=placed,
        out_specs=(
            P(("ctx", "tp"), "dp"),
            P(("ctx", "tp"), "dp"),
            P(("ctx", "tp"), "dp", None),
            P(("ctx", "tp"), "dp", None),
            P(("ctx", "tp"), "dp", None),
        ),
        check_vma=False,
    )
```

```python
import functools

import jax
import jax.numpy as jnp
from jax import lax
from jax.experimental import pallas as pl
from jax.experimental.pallas import tpu as pltpu
from jax.sharding import PartitionSpec as P

MESH = pl.DeviceIdType.MESH
F32 = jnp.float32
BF16 = jnp.bfloat16

NZ = 16
NY = 4
NX = 4
CAP = 6
BLOCK = 128
FOLD = 32
FEAT = 128
WIDE = 512
HID = 768
HALF = 384
ROWS = 192
PIECE = 48
OWN = 4
RING = (0, 1)


def mod(a, n):
    return lax.rem(a + 2 * n, n)


def nt(a, b):
    return lax.dot_general(a, b, (((1,), (1,)), ((), ())), preferred_element_type=F32)


def tn(a, b):
    return lax.dot_general(a, b, (((0,), (0,)), ((), ())), preferred_element_type=F32)


def nn(a, b):
    return jnp.dot(a, b, preferred_element_type=F32)


def body(
    ids_ref, codes_ref, tok_ref, grd_ref, wg_hbm, wu_hbm, wd_hbm,
    lo_ref, tg_ref, gg_hbm, ug_hbm, dg_hbm,
    data, meta_in, meta, wts, code_s, rank_s, gate_s, pick, pickg, ysend, rows_in,
    xs, core_out, core_in, part, opp_out, opp_in, back_out, back_in, fwd_out, fwd_in,
    gu, act, full, ret_out, ret_in, cmat, acc, rs_out, rs_in, wgrad,
    z_send, z_recv, my_send, my_recv, y_send, y_recv, c_send, c_recv,
    x_send, x_recv, g_send, g_recv, r_send, r_recv, s_send, s_recv, l_sem, w_sem, o_sem,
):
    dp = lax.axis_index("dp")
    z = lax.axis_index("ctx")
    y = lax.axis_index("tp")
    x = dp // 2
    core = dp - 2 * x
    z_nb = (mod(z + 1, NZ), mod(z - 1, NZ))
    z_nb2 = (mod(z + 2, NZ), mod(z - 2, NZ))
    x_right = mod(x + 1, NX)
    x_left = mod(x - 1, NX)
    x_opp = mod(x + 2, NX)
    peer = {"dp": 2 * x + 1 - core}

    barrier = pltpu.get_barrier_semaphore()
    for nb in z_nb + z_nb2:
        pl.semaphore_signal(barrier, inc=1, device_id={"ctx": nb}, device_id_type=MESH)
    for dy in range(1, NY):
        pl.semaphore_signal(barrier, inc=1, device_id={"tp": mod(y + dy, NY)}, device_id_type=MESH)
    for xn in (x_right, x_left):
        pl.semaphore_signal(barrier, inc=1, device_id={"dp": 2 * xn + core}, device_id_type=MESH)
    pl.semaphore_signal(barrier, inc=1, device_id=peer, device_id_type=MESH)

    own_copies = [
        pltpu.make_async_copy(tok_ref, data.at[0, OWN], l_sem.at[0]),
        pltpu.make_async_copy(grd_ref, data.at[1, OWN], l_sem.at[1]),
    ]
    w_copies = [
        pltpu.make_async_copy(w.at[0], wts.at[i], w_sem.at[i])
        for i, w in enumerate((wg_hbm, wu_hbm, wd_hbm))
    ]
    for cp in own_copies + w_copies:
        cp.start()
    small = jnp.concatenate([ids_ref[...].astype(F32), codes_ref[...].astype(F32)], axis=0)
    place = (
        lax.broadcasted_iota(jnp.int32, (FOLD, BLOCK), 1)
        == y * FOLD + lax.broadcasted_iota(jnp.int32, (FOLD, BLOCK), 0)
    )
    place = jnp.where(place, 1.0, 0.0).astype(BF16)
    meta_in[0] = nn(small.astype(BF16), place).astype(BF16)

    pl.semaphore_wait(barrier, 10)

    def at_distance(way, d):
        return (OWN - d) % NZ if way == 0 else (OWN + d) % NZ

    def zcopy(stream, way, d):
        hop = 2 if d % 2 == 0 else 1
        buf = meta if stream == 2 else data.at[stream]
        if d == hop and stream < 2:
            src = (tok_ref, grd_ref)[stream]
        else:
            src = buf.at[at_distance(way, d - hop)]
        return pltpu.make_async_remote_copy(
            src_ref=src, dst_ref=buf.at[at_distance(way, d)],
            send_sem=z_send.at[stream, way, d - 1], recv_sem=z_recv.at[stream, way, d - 1],
            device_id={"ctx": (z_nb, z_nb2)[hop - 1][way]}, device_id_type=MESH,
        )

    def reach(stream, way):
        return 8 if (stream == 1) == (way == 1) else 7

    def my_copy(dy):
        return pltpu.make_async_remote_copy(
            src_ref=meta_in.at[0], dst_ref=meta_in.at[dy],
            send_sem=my_send.at[dy - 1], recv_sem=my_recv.at[dy - 1],
            device_id={"tp": mod(y + dy, NY)}, device_id_type=MESH,
        )

    for dy in range(1, NY):
        my_copy(dy).start()
    toks = ((0, 0), (0, 1))
    grds = ((1, 1), (1, 0))
    routes = ((2, 0), (2, 1))
    for pairs in (toks, grds):
        for d in (2, 1):
            for pair in pairs:
                zcopy(*pair, d).start()
    for dy in range(1, NY):
        my_copy(dy).wait_recv()
    total = meta_in[0].astype(F32)
    for dy in range(1, NY):
        total = total + meta_in[dy].astype(F32)
    meta[OWN] = total.astype(BF16)
    for pair in routes:
        zcopy(*pair, 2).start()
        zcopy(*pair, 1).start()

    def relay(pairs, d):
        for pair in pairs:
            zcopy(*pair, d).wait_recv()
            if d + 2 <= reach(*pair):
                zcopy(*pair, d + 2).start()
        for pair in pairs:
            zcopy(*pair, d + 1).start()

    def arrived(pairs, first, last):
        for pair in pairs:
            for d in range(first, min(last, reach(*pair)) + 1):
                if d % 2 == 1 or d == 8:
                    zcopy(*pair, d).wait_recv()

    lane = lax.broadcasted_iota(jnp.int32, (32, BLOCK), 1)
    row = lax.broadcasted_iota(jnp.int32, (32, BLOCK), 0)

    def route(c):
        block = meta[8 * c:8 * c + 8].astype(F32)
        ids, gts = block[:, :8], block[:, 8:] * (1.0 / 256.0)
        ms, gs = [], []
        for dy in range(NY):
            e = (NY * z + mod(y + dy, NY)).astype(F32)
            hit = ids == e
            ms.append(jnp.sum(jnp.where(hit, 1.0, 0.0), axis=1))
            gs.append(jnp.sum(jnp.where(hit, gts, 0.0), axis=1))
        m = jnp.concatenate(ms, axis=0)
        g = jnp.concatenate(gs, axis=0)
        a = lax.broadcasted_iota(jnp.int32, (BLOCK, BLOCK), 0)
        b = lax.broadcasted_iota(jnp.int32, (BLOCK, BLOCK), 1)
        tri = jnp.where((a < b) & (a // FOLD == b // FOLD), 1.0, 0.0).astype(BF16)
        rank = nn(m.astype(BF16), tri)
        base = (lane // FOLD) * PIECE + (row % 8) * CAP
        code_s[c] = jnp.where(m > 0.5, base.astype(F32) + rank, -1.0)
        rank_s[c] = jnp.where(m > 0.5, rank + 1.0, 0.0)
        gate_s[c] = g

    def pickers(c):
        slot = lax.broadcasted_iota(jnp.int32, (ROWS, BLOCK), 0).astype(F32)

        def one(i, carry):
            hit = slot == code_s[c, pl.ds(i, 1), :]
            at = (
                c,
                pl.ds(pl.multiple_of((i // 8) * ROWS, ROWS), ROWS),
                pl.ds(pl.multiple_of((i % 8) * BLOCK, BLOCK), BLOCK),
            )
            pick[at] = jnp.where(hit, 1.0, 0.0).astype(BF16)
            pickg[at] = jnp.where(hit, gate_s[c, pl.ds(i, 1), :], 0.0).astype(BF16)
            return carry
        lax.fori_loop(0, 32, one, 0)

    def ycopy(c, dy, a):
        return pltpu.make_async_remote_copy(
            src_ref=ysend.at[c, dy, a], dst_ref=rows_in.at[c, y, a],
            send_sem=y_send.at[c, dy - 1, a], recv_sem=y_recv.at[c, dy - 1, a],
            device_id={"tp": mod(y + dy, NY)}, device_id_type=MESH,
        )

    def select(c, a):
        rows = data[a, 8 * c:8 * c + 8].reshape(8 * BLOCK, FEAT)
        picks = (pick, pickg)[a]
        for dy in (2, 1, 3, 0):
            got = nn(picks[c, dy * ROWS:(dy + 1) * ROWS, :], rows).astype(BF16)
            if dy == 0:
                rows_in[c, y, a] = got
            else:
                ysend[c, dy, a] = got
                ycopy(c, dy, a).start()

    def combiner(c):
        et = (
            lax.broadcasted_iota(jnp.int32, (FOLD, BLOCK), 1)
            == y * FOLD + lax.broadcasted_iota(jnp.int32, (FOLD, BLOCK), 0)
        )
        et = jnp.where(et, 1.0, 0.0).astype(BF16)
        rk = nt(et, rank_s[c].astype(BF16))
        gk = nt(et, gate_s[c].astype(BF16))
        col = lax.broadcasted_iota(jnp.int32, (FOLD, 32), 1)
        base = ((col // 8) * PIECE + (col % 8) * CAP - 1).astype(F32)
        tgt = jnp.where(rk > 0.5, base + rk, -1.0)
        out_lane = lax.broadcasted_iota(jnp.int32, (FOLD, ROWS), 1).astype(F32)
        for pp in range(8):
            ones = jnp.zeros((FOLD, ROWS), F32)
            gated = jnp.zeros((FOLD, ROWS), F32)
            for q in range(NY):
                k = q * 8 + pp
                hit = out_lane == tgt[:, k:k + 1]
                ones = jnp.where(hit, 1.0, ones)
                gated = jnp.where(hit, gk[:, k:k + 1], gated)
            cmat[c, 0, pp * FOLD:(pp + 1) * FOLD, :] = gated.astype(BF16)
            cmat[c, 1, pp * FOLD:(pp + 1) * FOLD, :] = ones.astype(BF16)

    mine = pl.ds(pl.multiple_of(core * HALF, HALF), HALF)
    other = pl.ds(pl.multiple_of((1 - core) * HALF, HALF), HALF)

    def core_copy(c, k):
        return pltpu.make_async_remote_copy(
            src_ref=core_out.at[c, k], dst_ref=core_in.at[c, k],
            send_sem=c_send.at[c, k], recv_sem=c_recv.at[c, k],
            device_id=peer, device_id_type=MESH,
        )

    def partials(c, a):
        at = slice(c * ROWS, (c + 1) * ROWS)
        for dy in range(1, NY):
            ycopy(c, dy, a).wait_recv()
        lhs = jnp.concatenate([rows_in[c, yy, a] for yy in range(NY)], axis=1)
        xs[a, at, :] = lhs
        for k in ((0, 1), (2,))[a]:
            core_out[c, k] = nn(lhs, wts[k, :, other]).astype(BF16)
            core_copy(c, k).start()
        for k in ((0, 1), (2,))[a]:
            part[c, k] = nn(lhs, wts[k, :, mine])

    def x_ends(c, k):
        return (x_right, x_left) if (c + k) % 2 == 0 else (x_left, x_right)

    def xcopy(c, kind, k):
        ahead, behind = x_ends(c, k)
        src, dst = ((opp_out, opp_in), (back_out, back_in), (fwd_out, fwd_in))[kind]
        to = behind if kind == 1 else ahead
        return pltpu.make_async_remote_copy(
            src_ref=src.at[c, k], dst_ref=dst.at[c, k],
            send_sem=x_send.at[c, kind, k], recv_sem=x_recv.at[c, kind, k],
            device_id={"dp": 2 * to + core}, device_id_type=MESH,
        )

    def piece(c, k, xx):
        at = pl.ds(pl.multiple_of(xx * PIECE, PIECE), PIECE)
        return part[c, k, at, :] + core_in[c, k, at, :].astype(F32)

    def x_first(c, k):
        core_copy(c, k).wait_recv()
        opp_out[c, k] = piece(c, k, x_opp).astype(BF16)
        xcopy(c, 0, k).start()
        back_out[c, k] = piece(c, k, x_ends(c, k)[1]).astype(BF16)
        xcopy(c, 1, k).start()

    def x_second(c, k):
        xcopy(c, 0, k).wait_recv()
        ahead = x_ends(c, k)[0]
        fwd_out[c, k] = (piece(c, k, ahead) + opp_in[c, k].astype(F32)).astype(BF16)
        xcopy(c, 2, k).start()

    def x_sum(c, k):
        xcopy(c, 1, k).wait_recv()
        xcopy(c, 2, k).wait_recv()
        return piece(c, k, x) + back_in[c, k].astype(F32) + fwd_in[c, k].astype(F32)

    def gcopy(c, j, k):
        ahead, behind = x_ends(c, k)
        slot = (x, x, x, behind, behind, ahead, x_opp)[j]
        to = (
            {"dp": 2 * ahead + core}, {"dp": 2 * behind + core}, peer,
            {"dp": 2 * ahead + core}, peer, peer, peer,
        )[j]
        return pltpu.make_async_remote_copy(
            src_ref=act.at[c, k, core, slot], dst_ref=act.at[c, k, core, slot],
            send_sem=g_send.at[c, k, j], recv_sem=g_recv.at[c, k, j],
            device_id=to, device_id_type=MESH,
        )

    def spread(c, k):
        for j in (0, 1, 2):
            gcopy(c, j, k).start()

    def forward(c):
        pre_gate, pre_up = x_sum(c, 0), x_sum(c, 1)
        gu[c, 0] = pre_gate
        gu[c, 1] = pre_up
        act[c, 0, core, x] = (pre_gate * jax.nn.sigmoid(pre_gate) * pre_up).astype(BF16)
        spread(c, 0)

    def backward(c):
        hid_grad = x_sum(c, 2)
        pre_gate, pre_up = gu[c, 0], gu[c, 1]
        squash = jax.nn.sigmoid(pre_gate)
        act[c, 1, core, x] = (
            hid_grad * pre_up * squash * (1.0 + pre_gate * (1.0 - squash))
        ).astype(BF16)
        spread(c, 1)
        act[c, 2, core, x] = (hid_grad * pre_gate * squash).astype(BF16)
        spread(c, 2)

    def gather(c, k):
        gcopy(c, 0, k).wait_recv()
        gcopy(c, 3, k).start()
        gcopy(c, 4, k).start()
        gcopy(c, 1, k).wait_recv()
        gcopy(c, 5, k).start()

    def gather_end(c, k):
        gcopy(c, 3, k).wait_recv()
        gcopy(c, 6, k).start()
        for j in (2, 4, 5, 6):
            gcopy(c, j, k).wait_recv()

    def rcopy(c, dy, a):
        return pltpu.make_async_remote_copy(
            src_ref=ret_out.at[c, mod(y + dy, NY), a], dst_ref=ret_in.at[c, NY - dy, a],
            send_sem=r_send.at[c, dy - 1, a], recv_sem=r_recv.at[c, dy - 1, a],
            device_id={"tp": mod(y + dy, NY)}, device_id_type=MESH,
        )

    def results(c, a):
        at = slice(c * ROWS, (c + 1) * ROWS)
        for k in ((0,), (1, 2))[a]:
            for h in (0, 1):
                full[k, at, h * HALF:(h + 1) * HALF] = act[c, k, h].reshape(ROWS, HALF)
        if a == 0:
            value = nt(full[0, at, :], wts[2])
        else:
            value = nt(full[1, at, :], wts[0]) + nt(full[2, at, :], wts[1])
        ret_out[c, :, a] = value.astype(BF16).reshape(NY, PIECE, WIDE)
        for dy in (2, 1, 3):
            rcopy(c, dy, a).start()
        ret_in[c, 0, a] = ret_out[c, y, a]

    def combine(c, a):
        for dy in range(1, NY):
            rcopy(c, dy, a).wait_recv()
        got = ret_in[c, :, a].reshape(ROWS, WIDE)
        acc[a, 256 * c:256 * c + 256, :] = nn(cmat[c, a], got)

    def weight_grad(k):
        lhs = xs[k // 2]
        rhs = full[(1, 2, 0)[k]]
        wgrad[k] = tn(lhs, rhs).astype(BF16)
        pltpu.make_async_copy(wgrad.at[k], (gg_hbm, ug_hbm, dg_hbm)[k].at[0], o_sem.at[k]).start()

    def scopy(a, way, d):
        hop = 2 if d % 2 == 0 else 1
        return pltpu.make_async_remote_copy(
            src_ref=rs_out.at[a, way, d - 1], dst_ref=rs_in.at[a, way, d - 1],
            send_sem=s_send.at[a, way, d - 1], recv_sem=s_recv.at[a, way, d - 1],
            device_id={"ctx": (z_nb, z_nb2)[hop - 1][way]}, device_id_type=MESH,
        )

    def span(a, way):
        return 8 if a == way else 7

    def collected(a, way, d):
        p = (OWN + d) % NZ if way == 0 else (OWN - d) % NZ
        value = acc[a, p * FOLD:(p + 1) * FOLD, :]
        if d % 2 == 0:
            for e in (d + 1, d + 2):
                if e <= span(a, way):
                    scopy(a, way, e).wait_recv()
                    value = value + rs_in[a, way, e - 1].astype(F32)
        return value

    def send_sums(a, *ds):
        for d in ds:
            for way in RING:
                if d <= span(a, way):
                    rs_out[a, way, d - 1] = collected(a, way, d).astype(BF16)
                    scopy(a, way, d).start()

    relay(toks, 2)
    relay(routes, 2)
    relay(grds, 2)
    relay(toks, 4)
    relay(routes, 4)
    relay(grds, 4)
    arrived(routes, 1, 4)
    route(0)
    pickers(0)
    relay(toks, 6)
    relay(routes, 6)
    for cp in own_copies:
        cp.wait()
    arrived(toks, 1, 4)
    select(0, 0)
    relay(grds, 6)
    arrived(grds, 1, 4)
    select(0, 1)
    arrived(routes, 5, 8)
    route(1)
    pickers(1)
    arrived(toks, 5, 8)
    select(1, 0)
    for cp in w_copies:
        cp.wait()
    partials(0, 0)
    arrived(grds, 5, 8)
    select(1, 1)
    x_first(0, 0)
    x_first(0, 1)
    partials(0, 1)
    x_first(0, 2)
    partials(1, 0)
    x_second(0, 0)
    x_second(0, 1)
    x_first(1, 0)
    x_first(1, 1)
    x_second(0, 2)
    partials(1, 1)
    x_first(1, 2)
    forward(0)
    x_second(1, 0)
    x_second(1, 1)
    backward(0)
    x_second(1, 2)
    gather(0, 0)
    forward(1)
    gather(0, 1)
    gather(0, 2)
    backward(1)
    gather_end(0, 0)
    gather(1, 0)
    gather_end(0, 1)
    gather_end(0, 2)
    results(0, 0)
    gather(1, 1)
    gather(1, 2)
    gather_end(1, 0)
    results(1, 0)
    results(0, 1)
    combiner(0)
    combiner(1)
    gather_end(1, 1)
    gather_end(1, 2)
    results(1, 1)
    combine(0, 0)
    combine(1, 0)
    send_sums(0, 8, 7)
    combine(0, 1)
    combine(1, 1)
    send_sums(1, 8, 7)
    weight_grad(2)
    send_sums(0, 6, 5)
    weight_grad(0)
    send_sums(1, 6, 5)
    weight_grad(1)
    send_sums(0, 4, 3)
    send_sums(1, 4, 3)

    for dy in range(1, NY):
        my_copy(dy).wait_send()
        for c in (0, 1):
            for a in (0, 1):
                ycopy(c, dy, a).wait_send()
                rcopy(c, dy, a).wait_send()
    send_sums(0, 2, 1)
    send_sums(1, 2, 1)
    for pair in routes + toks + grds:
        for d in range(1, reach(*pair) + 1):
            zcopy(*pair, d).wait_send()
    for c in (0, 1):
        for k in range(3):
            core_copy(c, k).wait_send()
            for kind in range(3):
                xcopy(c, kind, k).wait_send()
            for j in range(7):
                gcopy(c, j, k).wait_send()

    for a, ref in ((0, lo_ref), (1, tg_ref)):
        value = acc[a, OWN * FOLD:(OWN + 1) * FOLD, :]
        for way in RING:
            for d in (1, 2):
                scopy(a, way, d).wait_recv()
                value = value + rs_in[a, way, d - 1].astype(F32)
        ref[...] = value.astype(BF16)
    for a in (0, 1):
        for way in RING:
            for d in range(1, span(a, way) + 1):
                scopy(a, way, d).wait_send()
    for k in range(3):
        pltpu.make_async_copy(
            wgrad.at[k], (gg_hbm, ug_hbm, dg_hbm)[k].at[0], o_sem.at[k]
        ).wait()


def keep_body(*refs):
    sources, results, held, sems = refs[:5], refs[5:10], refs[10:15], refs[15]
    into = [pltpu.make_async_copy(sources[i], held[i], sems.at[0, i]) for i in range(5)]
    out = [pltpu.make_async_copy(held[i], results[i], sems.at[1, i]) for i in range(5)]
    for cp in into:
        cp.start()
    for first, second in zip(into, out):
        first.wait()
        second.start()
    for cp in out:
        cp.wait()


def shards(tokens, expert_ids, gate_codes, gate_weight, up_weight, down_weight, out_grad):
    vmem = pl.BlockSpec(memory_space=pltpu.VMEM)
    hbm = pl.BlockSpec(memory_space=pltpu.HBM)
    dma = pltpu.SemaphoreType.DMA
    scratch = [
        pltpu.VMEM((2, NZ, BLOCK, FEAT), BF16),
        pltpu.VMEM((NY, 16, BLOCK), BF16),
        pltpu.VMEM((NZ, 16, BLOCK), BF16),
        pltpu.VMEM((3, WIDE, HID), BF16),
        pltpu.VMEM((2, 32, BLOCK), F32),
        pltpu.VMEM((2, 32, BLOCK), F32),
        pltpu.VMEM((2, 32, BLOCK), F32),
        pltpu.VMEM((2, NY * ROWS, 8 * BLOCK), BF16),
        pltpu.VMEM((2, NY * ROWS, 8 * BLOCK), BF16),
        pltpu.VMEM((2, NY, 2, ROWS, FEAT), BF16),
        pltpu.VMEM((2, NY, 2, ROWS, FEAT), BF16),
        pltpu.VMEM((2, 2 * ROWS, WIDE), BF16),
        pltpu.VMEM((2, 3, ROWS, HALF), BF16),
        pltpu.VMEM((2, 3, ROWS, HALF), BF16),
        pltpu.VMEM((2, 3, ROWS, HALF), F32),
    ] + [pltpu.VMEM((2, 3, PIECE, HALF), BF16)] * 6 + [
        pltpu.VMEM((2, 2, PIECE, HALF), F32),
        pltpu.VMEM((2, 3, 2, NX, PIECE, HALF), BF16),
        pltpu.VMEM((3, 2 * ROWS, HID), BF16),
        pltpu.VMEM((2, NY, 2, PIECE, WIDE), BF16),
        pltpu.VMEM((2, NY, 2, PIECE, WIDE), BF16),
        pltpu.VMEM((2, 2, 8 * FOLD, ROWS), BF16),
        pltpu.VMEM((2, NZ * FOLD, WIDE), F32),
        pltpu.VMEM((2, 2, 8, FOLD, WIDE), BF16),
        pltpu.VMEM((2, 2, 8, FOLD, WIDE), BF16),
        pltpu.VMEM((3, WIDE, HID), BF16),
        dma((3, 2, 8)), dma((3, 2, 8)),
        dma((3,)), dma((3,)),
        dma((2, 3, 2)), dma((2, 3, 2)),
        dma((2, 3)), dma((2, 3)),
        dma((2, 3, 3)), dma((2, 3, 3)),
        dma((2, 3, 7)), dma((2, 3, 7)),
        dma((2, 3, 2)), dma((2, 3, 2)),
        dma((2, 2, 8)), dma((2, 2, 8)),
        dma((2,)), dma((3,)), dma((3,)),
    ]
    fold = jax.ShapeDtypeStruct((FOLD, WIDE), BF16)
    weight = jax.ShapeDtypeStruct((1, WIDE, HID), BF16)
    hbm5 = (hbm,) * 5
    results = pl.pallas_call(
        body,
        out_shape=(fold, fold, weight, weight, weight),
        in_specs=[vmem, vmem, hbm, hbm, hbm, hbm, hbm],
        out_specs=(vmem, vmem, hbm, hbm, hbm),
        scratch_shapes=scratch,
        compiler_params=pltpu.CompilerParams(
            collective_id=0, has_side_effects=True, vmem_limit_bytes=56 * 1024 * 1024
        ),
    )(
        expert_ids.T, gate_codes.T, tokens, out_grad, gate_weight, up_weight, down_weight
    )
    return pl.pallas_call(
        keep_body,
        out_shape=(fold, fold, weight, weight, weight),
        in_specs=hbm5,
        out_specs=hbm5,
        scratch_shapes=[pltpu.VMEM(out.shape, BF16) for out in (fold, fold, weight, weight, weight)]
        + [dma((2, 5))],
    )(*results)


def solution(mesh):
    placed = (
        P("ctx", ("dp", "tp")),
        P(("ctx", "tp"), None),
        P(("ctx", "tp"), None),
        P(("ctx", "tp"), "dp", None),
        P(("ctx", "tp"), "dp", None),
        P(("ctx", "tp"), "dp", None),
        P("ctx", ("dp", "tp")),
    )
    return jax.shard_map(
        shards,
        mesh=mesh,
        in_specs=placed,
        out_specs=(
            P(("ctx", "tp"), "dp"),
            P(("ctx", "tp"), "dp"),
            P(("ctx", "tp"), "dp", None),
            P(("ctx", "tp"), "dp", None),
            P(("ctx", "tp"), "dp", None),
        ),
        check_vma=False,
    )
```

```python
import functools

import jax
import jax.numpy as jnp
from jax import lax
from jax.experimental import pallas as pl
from jax.experimental.pallas import tpu as pltpu
from jax.sharding import PartitionSpec as P

MESH = pl.DeviceIdType.MESH
F32 = jnp.float32
BF16 = jnp.bfloat16

NZ = 16
NY = 4
NX = 4
CAP = 6
BLOCK = 128
FOLD = 32
FEAT = 128
WIDE = 512
HID = 768
HALF = 384
ROWS = 192
PIECE = 48
OWN = 4
RING = (0, 1)


def mod(a, n):
    return lax.rem(a + 2 * n, n)


def nt(a, b):
    return lax.dot_general(a, b, (((1,), (1,)), ((), ())), preferred_element_type=F32)


def tn(a, b):
    return lax.dot_general(a, b, (((0,), (0,)), ((), ())), preferred_element_type=F32)


def nn(a, b):
    return jnp.dot(a, b, preferred_element_type=F32)


def body(
    ids_ref, codes_ref, tok_ref, grd_ref, wg_hbm, wu_hbm, wd_hbm,
    lo_ref, tg_ref, gg_hbm, ug_hbm, dg_hbm,
    data, meta_in, meta, wts, code_s, rank_s, gate_s, pick, pickg, ysend, rows_in,
    xs, core_out, core_in, part, opp_out, opp_in, back_out, back_in, fwd_out, fwd_in,
    gu, act, full, ret_out, ret_in, cmat, acc, rs_out, rs_in, wgrad,
    z_send, z_recv, my_send, my_recv, y_send, y_recv, c_send, c_recv,
    x_send, x_recv, g_send, g_recv, r_send, r_recv, s_send, s_recv, l_sem, w_sem, o_sem,
):
    dp = lax.axis_index("dp")
    z = lax.axis_index("ctx")
    y = lax.axis_index("tp")
    x = dp // 2
    core = dp - 2 * x
    z_nb = (mod(z + 1, NZ), mod(z - 1, NZ))
    z_nb2 = (mod(z + 2, NZ), mod(z - 2, NZ))
    x_right = mod(x + 1, NX)
    x_left = mod(x - 1, NX)
    x_opp = mod(x + 2, NX)
    peer = {"dp": 2 * x + 1 - core}

    barrier = pltpu.get_barrier_semaphore()
    for nb in z_nb + z_nb2:
        pl.semaphore_signal(barrier, inc=1, device_id={"ctx": nb}, device_id_type=MESH)
    for dy in range(1, NY):
        pl.semaphore_signal(barrier, inc=1, device_id={"tp": mod(y + dy, NY)}, device_id_type=MESH)
    for xn in (x_right, x_left):
        pl.semaphore_signal(barrier, inc=1, device_id={"dp": 2 * xn + core}, device_id_type=MESH)
    pl.semaphore_signal(barrier, inc=1, device_id=peer, device_id_type=MESH)

    own_copies = [
        pltpu.make_async_copy(tok_ref, data.at[0, OWN], l_sem.at[0]),
        pltpu.make_async_copy(grd_ref, data.at[1, OWN], l_sem.at[1]),
    ]
    w_copies = [
        pltpu.make_async_copy(w.at[0], wts.at[i], w_sem.at[i])
        for i, w in enumerate((wg_hbm, wu_hbm, wd_hbm))
    ]
    for cp in own_copies + w_copies:
        cp.start()
    small = jnp.concatenate([ids_ref[...].astype(F32), codes_ref[...].astype(F32)], axis=0)
    place = (
        lax.broadcasted_iota(jnp.int32, (FOLD, BLOCK), 1)
        == y * FOLD + lax.broadcasted_iota(jnp.int32, (FOLD, BLOCK), 0)
    )
    place = jnp.where(place, 1.0, 0.0).astype(BF16)
    meta_in[0] = nn(small.astype(BF16), place).astype(BF16)

    pl.semaphore_wait(barrier, 10)

    def at_distance(way, d):
        return (OWN - d) % NZ if way == 0 else (OWN + d) % NZ

    def zcopy(stream, way, d):
        hop = 2 if d % 2 == 0 else 1
        buf = meta if stream == 2 else data.at[stream]
        if d == hop and stream < 2:
            src = (tok_ref, grd_ref)[stream]
        else:
            src = buf.at[at_distance(way, d - hop)]
        return pltpu.make_async_remote_copy(
            src_ref=src, dst_ref=buf.at[at_distance(way, d)],
            send_sem=z_send.at[stream, way, d - 1], recv_sem=z_recv.at[stream, way, d - 1],
            device_id={"ctx": (z_nb, z_nb2)[hop - 1][way]}, device_id_type=MESH,
        )

    def reach(stream, way):
        return 8 if (stream == 1) == (way == 1) else 7

    def my_copy(dy):
        return pltpu.make_async_remote_copy(
            src_ref=meta_in.at[0], dst_ref=meta_in.at[dy],
            send_sem=my_send.at[dy - 1], recv_sem=my_recv.at[dy - 1],
            device_id={"tp": mod(y + dy, NY)}, device_id_type=MESH,
        )

    for dy in range(1, NY):
        my_copy(dy).start()
    toks = ((0, 0), (0, 1))
    grds = ((1, 1), (1, 0))
    routes = ((2, 0), (2, 1))
    for pairs in (toks, grds):
        for d in (2, 1):
            for pair in pairs:
                zcopy(*pair, d).start()
    for dy in range(1, NY):
        my_copy(dy).wait_recv()
    total = meta_in[0].astype(F32)
    for dy in range(1, NY):
        total = total + meta_in[dy].astype(F32)
    meta[OWN] = total.astype(BF16)
    for pair in routes:
        zcopy(*pair, 2).start()
        zcopy(*pair, 1).start()

    def relay(pairs, d):
        for pair in pairs:
            zcopy(*pair, d).wait_recv()
            if d + 2 <= reach(*pair):
                zcopy(*pair, d + 2).start()
        for pair in pairs:
            zcopy(*pair, d + 1).start()

    def arrived(pairs, first, last):
        for pair in pairs:
            for d in range(first, min(last, reach(*pair)) + 1):
                if d % 2 == 1 or d == 8:
                    zcopy(*pair, d).wait_recv()

    lane = lax.broadcasted_iota(jnp.int32, (32, BLOCK), 1)
    row = lax.broadcasted_iota(jnp.int32, (32, BLOCK), 0)

    def route(c):
        block = meta[8 * c:8 * c + 8].astype(F32)
        ids, gts = block[:, :8], block[:, 8:] * (1.0 / 256.0)
        ms, gs = [], []
        for dy in range(NY):
            e = (NY * z + mod(y + dy, NY)).astype(F32)
            hit = ids == e
            ms.append(jnp.sum(jnp.where(hit, 1.0, 0.0), axis=1))
            gs.append(jnp.sum(jnp.where(hit, gts, 0.0), axis=1))
        m = jnp.concatenate(ms, axis=0)
        g = jnp.concatenate(gs, axis=0)
        a = lax.broadcasted_iota(jnp.int32, (BLOCK, BLOCK), 0)
        b = lax.broadcasted_iota(jnp.int32, (BLOCK, BLOCK), 1)
        tri = jnp.where((a < b) & (a // FOLD == b // FOLD), 1.0, 0.0).astype(BF16)
        rank = nn(m.astype(BF16), tri)
        base = (lane // FOLD) * PIECE + (row % 8) * CAP
        code_s[c] = jnp.where(m > 0.5, base.astype(F32) + rank, -1.0)
        rank_s[c] = jnp.where(m > 0.5, rank + 1.0, 0.0)
        gate_s[c] = g

    def pickers(c):
        slot = lax.broadcasted_iota(jnp.int32, (ROWS, BLOCK), 0).astype(F32)

        def one(i, carry):
            hit = slot == code_s[c, pl.ds(i, 1), :]
            at = (
                c,
                pl.ds(pl.multiple_of((i // 8) * ROWS, ROWS), ROWS),
                pl.ds(pl.multiple_of((i % 8) * BLOCK, BLOCK), BLOCK),
            )
            pick[at] = jnp.where(hit, 1.0, 0.0).astype(BF16)
            pickg[at] = jnp.where(hit, gate_s[c, pl.ds(i, 1), :], 0.0).astype(BF16)
            return carry
        lax.fori_loop(0, 32, one, 0)

    def ycopy(c, dy, a):
        return pltpu.make_async_remote_copy(
            src_ref=ysend.at[c, dy, a], dst_ref=rows_in.at[c, y, a],
            send_sem=y_send.at[c, dy - 1, a], recv_sem=y_recv.at[c, dy - 1, a],
            device_id={"tp": mod(y + dy, NY)}, device_id_type=MESH,
        )

    def select(c, a):
        rows = data[a, 8 * c:8 * c + 8].reshape(8 * BLOCK, FEAT)
        picks = (pick, pickg)[a]
        for dy in (2, 1, 3, 0):
            got = nn(picks[c, dy * ROWS:(dy + 1) * ROWS, :], rows).astype(BF16)
            if dy == 0:
                rows_in[c, y, a] = got
            else:
                ysend[c, dy, a] = got
                ycopy(c, dy, a).start()

    def combiner(c):
        et = (
            lax.broadcasted_iota(jnp.int32, (FOLD, BLOCK), 1)
            == y * FOLD + lax.broadcasted_iota(jnp.int32, (FOLD, BLOCK), 0)
        )
        et = jnp.where(et, 1.0, 0.0).astype(BF16)
        rk = nt(et, rank_s[c].astype(BF16))
        gk = nt(et, gate_s[c].astype(BF16))
        col = lax.broadcasted_iota(jnp.int32, (FOLD, 32), 1)
        base = ((col // 8) * PIECE + (col % 8) * CAP - 1).astype(F32)
        tgt = jnp.where(rk > 0.5, base + rk, -1.0)
        out_lane = lax.broadcasted_iota(jnp.int32, (FOLD, ROWS), 1).astype(F32)
        for pp in range(8):
            ones = jnp.zeros((FOLD, ROWS), F32)
            gated = jnp.zeros((FOLD, ROWS), F32)
            for q in range(NY):
                k = q * 8 + pp
                hit = out_lane == tgt[:, k:k + 1]
                ones = jnp.where(hit, 1.0, ones)
                gated = jnp.where(hit, gk[:, k:k + 1], gated)
            cmat[c, 0, pp * FOLD:(pp + 1) * FOLD, :] = gated.astype(BF16)
            cmat[c, 1, pp * FOLD:(pp + 1) * FOLD, :] = ones.astype(BF16)

    mine = pl.ds(pl.multiple_of(core * HALF, HALF), HALF)
    other = pl.ds(pl.multiple_of((1 - core) * HALF, HALF), HALF)

    def core_copy(c, k):
        return pltpu.make_async_remote_copy(
            src_ref=core_out.at[c, k], dst_ref=core_in.at[c, k],
            send_sem=c_send.at[c, k], recv_sem=c_recv.at[c, k],
            device_id=peer, device_id_type=MESH,
        )

    def partials(c, a):
        at = slice(c * ROWS, (c + 1) * ROWS)
        for dy in range(1, NY):
            ycopy(c, dy, a).wait_recv()
        lhs = jnp.concatenate([rows_in[c, yy, a] for yy in range(NY)], axis=1)
        xs[a, at, :] = lhs
        for k in ((0, 1), (2,))[a]:
            core_out[c, k] = nn(lhs, wts[k, :, other]).astype(BF16)
            core_copy(c, k).start()
        for k in ((0, 1), (2,))[a]:
            part[c, k] = nn(lhs, wts[k, :, mine])

    def x_ends(c, k):
        return (x_right, x_left) if (c + k) % 2 == 0 else (x_left, x_right)

    def xcopy(c, kind, k):
        ahead, behind = x_ends(c, k)
        src, dst = ((opp_out, opp_in), (back_out, back_in), (fwd_out, fwd_in))[kind]
        to = behind if kind == 1 else ahead
        return pltpu.make_async_remote_copy(
            src_ref=src.at[c, k], dst_ref=dst.at[c, k],
            send_sem=x_send.at[c, kind, k], recv_sem=x_recv.at[c, kind, k],
            device_id={"dp": 2 * to + core}, device_id_type=MESH,
        )

    def piece(c, k, xx):
        at = pl.ds(pl.multiple_of(xx * PIECE, PIECE), PIECE)
        return part[c, k, at, :] + core_in[c, k, at, :].astype(F32)

    def x_first(c, k):
        core_copy(c, k).wait_recv()
        opp_out[c, k] = piece(c, k, x_opp).astype(BF16)
        xcopy(c, 0, k).start()
        back_out[c, k] = piece(c, k, x_ends(c, k)[1]).astype(BF16)
        xcopy(c, 1, k).start()

    def x_second(c, k):
        xcopy(c, 0, k).wait_recv()
        ahead = x_ends(c, k)[0]
        fwd_out[c, k] = (piece(c, k, ahead) + opp_in[c, k].astype(F32)).astype(BF16)
        xcopy(c, 2, k).start()

    def x_sum(c, k):
        xcopy(c, 1, k).wait_recv()
        xcopy(c, 2, k).wait_recv()
        return piece(c, k, x) + back_in[c, k].astype(F32) + fwd_in[c, k].astype(F32)

    def gcopy(c, j, k):
        ahead, behind = x_ends(c, k)
        slot = (x, x, x, behind, behind, ahead, x_opp)[j]
        to = (
            {"dp": 2 * ahead + core}, {"dp": 2 * behind + core}, peer,
            {"dp": 2 * ahead + core}, peer, peer, peer,
        )[j]
        return pltpu.make_async_remote_copy(
            src_ref=act.at[c, k, core, slot], dst_ref=act.at[c, k, core, slot],
            send_sem=g_send.at[c, k, j], recv_sem=g_recv.at[c, k, j],
            device_id=to, device_id_type=MESH,
        )

    def spread(c, k):
        for j in (0, 1, 2):
            gcopy(c, j, k).start()

    def forward(c):
        pre_gate, pre_up = x_sum(c, 0), x_sum(c, 1)
        gu[c, 0] = pre_gate
        gu[c, 1] = pre_up
        act[c, 0, core, x] = (pre_gate * jax.nn.sigmoid(pre_gate) * pre_up).astype(BF16)
        spread(c, 0)

    def backward(c):
        hid_grad = x_sum(c, 2)
        pre_gate, pre_up = gu[c, 0], gu[c, 1]
        squash = jax.nn.sigmoid(pre_gate)
        act[c, 1, core, x] = (
            hid_grad * pre_up * squash * (1.0 + pre_gate * (1.0 - squash))
        ).astype(BF16)
        spread(c, 1)
        act[c, 2, core, x] = (hid_grad * pre_gate * squash).astype(BF16)
        spread(c, 2)

    def gather(c, k):
        gcopy(c, 0, k).wait_recv()
        gcopy(c, 3, k).start()
        gcopy(c, 4, k).start()
        gcopy(c, 1, k).wait_recv()
        gcopy(c, 5, k).start()

    def gather_end(c, k):
        gcopy(c, 3, k).wait_recv()
        gcopy(c, 6, k).start()
        for j in (2, 4, 5, 6):
            gcopy(c, j, k).wait_recv()

    def rcopy(c, dy, a):
        return pltpu.make_async_remote_copy(
            src_ref=ret_out.at[c, mod(y + dy, NY), a], dst_ref=ret_in.at[c, NY - dy, a],
            send_sem=r_send.at[c, dy - 1, a], recv_sem=r_recv.at[c, dy - 1, a],
            device_id={"tp": mod(y + dy, NY)}, device_id_type=MESH,
        )

    def results(c, a):
        at = slice(c * ROWS, (c + 1) * ROWS)
        for k in ((0,), (1, 2))[a]:
            for h in (0, 1):
                full[k, at, h * HALF:(h + 1) * HALF] = act[c, k, h].reshape(ROWS, HALF)
        if a == 0:
            value = nt(full[0, at, :], wts[2])
        else:
            value = nt(full[1, at, :], wts[0]) + nt(full[2, at, :], wts[1])
        ret_out[c, :, a] = value.astype(BF16).reshape(NY, PIECE, WIDE)
        for dy in (2, 1, 3):
            rcopy(c, dy, a).start()
        ret_in[c, 0, a] = ret_out[c, y, a]

    def combine(c, a):
        for dy in range(1, NY):
            rcopy(c, dy, a).wait_recv()
        got = ret_in[c, :, a].reshape(ROWS, WIDE)
        acc[a, 256 * c:256 * c + 256, :] = nn(cmat[c, a], got)

    def weight_grad(k):
        lhs = xs[k // 2]
        rhs = full[(1, 2, 0)[k]]
        wgrad[k] = tn(lhs, rhs).astype(BF16)
        pltpu.make_async_copy(wgrad.at[k], (gg_hbm, ug_hbm, dg_hbm)[k].at[0], o_sem.at[k]).start()

    def scopy(a, way, d):
        hop = 2 if d % 2 == 0 else 1
        return pltpu.make_async_remote_copy(
            src_ref=rs_out.at[a, way, d - 1], dst_ref=rs_in.at[a, way, d - 1],
            send_sem=s_send.at[a, way, d - 1], recv_sem=s_recv.at[a, way, d - 1],
            device_id={"ctx": (z_nb, z_nb2)[hop - 1][way]}, device_id_type=MESH,
        )

    def span(a, way):
        return 8 if a == way else 7

    def collected(a, way, d):
        p = (OWN + d) % NZ if way == 0 else (OWN - d) % NZ
        value = acc[a, p * FOLD:(p + 1) * FOLD, :]
        if d % 2 == 0:
            for e in (d + 1, d + 2):
                if e <= span(a, way):
                    scopy(a, way, e).wait_recv()
                    value = value + rs_in[a, way, e - 1].astype(F32)
        return value

    def send_sums(a, *ds):
        for d in ds:
            for way in RING:
                if d <= span(a, way):
                    rs_out[a, way, d - 1] = collected(a, way, d).astype(BF16)
                    scopy(a, way, d).start()

    relay(toks, 2)
    relay(routes, 2)
    relay(grds, 2)
    relay(toks, 4)
    relay(routes, 4)
    relay(grds, 4)
    arrived(routes, 1, 4)
    route(0)
    pickers(0)
    relay(toks, 6)
    relay(routes, 6)
    for cp in own_copies:
        cp.wait()
    arrived(toks, 1, 4)
    select(0, 0)
    relay(grds, 6)
    arrived(grds, 1, 4)
    select(0, 1)
    arrived(routes, 5, 8)
    route(1)
    pickers(1)
    arrived(toks, 5, 8)
    select(1, 0)
    for cp in w_copies:
        cp.wait()
    partials(0, 0)
    arrived(grds, 5, 8)
    select(1, 1)
    x_first(0, 0)
    x_first(0, 1)
    partials(0, 1)
    x_first(0, 2)
    partials(1, 0)
    x_second(0, 0)
    x_second(0, 1)
    x_first(1, 0)
    x_first(1, 1)
    x_second(0, 2)
    partials(1, 1)
    x_first(1, 2)
    combiner(0)
    forward(0)
    combiner(1)
    x_second(1, 0)
    x_second(1, 1)
    backward(0)
    x_second(1, 2)
    gather(0, 0)
    forward(1)
    gather(0, 1)
    gather(0, 2)
    backward(1)
    gather_end(0, 0)
    gather(1, 0)
    gather_end(0, 1)
    gather_end(0, 2)
    results(0, 0)
    gather(1, 1)
    gather(1, 2)
    gather_end(1, 0)
    results(1, 0)
    results(0, 1)
    gather_end(1, 1)
    gather_end(1, 2)
    results(1, 1)
    combine(0, 0)
    combine(1, 0)
    send_sums(0, 8, 7)
    combine(0, 1)
    weight_grad(2)
    weight_grad(0)
    weight_grad(1)
    combine(1, 1)
    send_sums(1, 8, 7)
    send_sums(0, 6, 5)
    send_sums(1, 6, 5)
    send_sums(0, 4, 3)
    send_sums(1, 4, 3)

    for dy in range(1, NY):
        my_copy(dy).wait_send()
        for c in (0, 1):
            for a in (0, 1):
                ycopy(c, dy, a).wait_send()
                rcopy(c, dy, a).wait_send()
    send_sums(0, 2, 1)
    send_sums(1, 2, 1)
    for pair in routes + toks + grds:
        for d in range(1, reach(*pair) + 1):
            zcopy(*pair, d).wait_send()
    for c in (0, 1):
        for k in range(3):
            core_copy(c, k).wait_send()
            for kind in range(3):
                xcopy(c, kind, k).wait_send()
            for j in range(7):
                gcopy(c, j, k).wait_send()

    for a, ref in ((0, lo_ref), (1, tg_ref)):
        value = acc[a, OWN * FOLD:(OWN + 1) * FOLD, :]
        for way in RING:
            for d in (1, 2):
                scopy(a, way, d).wait_recv()
                value = value + rs_in[a, way, d - 1].astype(F32)
        ref[...] = value.astype(BF16)
    for a in (0, 1):
        for way in RING:
            for d in range(1, span(a, way) + 1):
                scopy(a, way, d).wait_send()
    for k in range(3):
        pltpu.make_async_copy(
            wgrad.at[k], (gg_hbm, ug_hbm, dg_hbm)[k].at[0], o_sem.at[k]
        ).wait()


def keep_body(*refs):
    sources, results, held, sems = refs[:5], refs[5:10], refs[10:15], refs[15]
    parts = [(0, pl.ds(0, FOLD)), (1, pl.ds(0, FOLD))]
    parts += [(i, (0, pl.ds(h * 256, 256))) for i in (2, 3, 4) for h in (0, 1)]
    into = [
        pltpu.make_async_copy(sources[i].at[at], held[i].at[at], sems.at[0, n])
        for n, (i, at) in enumerate(parts)
    ]
    out = [
        pltpu.make_async_copy(held[i].at[at], results[i].at[at], sems.at[1, n])
        for n, (i, at) in enumerate(parts)
    ]
    for cp in into:
        cp.start()
    for first, second in zip(into, out):
        first.wait()
        second.start()
    for cp in out:
        cp.wait()


def shards(tokens, expert_ids, gate_codes, gate_weight, up_weight, down_weight, out_grad):
    vmem = pl.BlockSpec(memory_space=pltpu.VMEM)
    hbm = pl.BlockSpec(memory_space=pltpu.HBM)
    dma = pltpu.SemaphoreType.DMA
    scratch = [
        pltpu.VMEM((2, NZ, BLOCK, FEAT), BF16),
        pltpu.VMEM((NY, 16, BLOCK), BF16),
        pltpu.VMEM((NZ, 16, BLOCK), BF16),
        pltpu.VMEM((3, WIDE, HID), BF16),
        pltpu.VMEM((2, 32, BLOCK), F32),
        pltpu.VMEM((2, 32, BLOCK), F32),
        pltpu.VMEM((2, 32, BLOCK), F32),
        pltpu.VMEM((2, NY * ROWS, 8 * BLOCK), BF16),
        pltpu.VMEM((2, NY * ROWS, 8 * BLOCK), BF16),
        pltpu.VMEM((2, NY, 2, ROWS, FEAT), BF16),
        pltpu.VMEM((2, NY, 2, ROWS, FEAT), BF16),
        pltpu.VMEM((2, 2 * ROWS, WIDE), BF16),
        pltpu.VMEM((2, 3, ROWS, HALF), BF16),
        pltpu.VMEM((2, 3, ROWS, HALF), BF16),
        pltpu.VMEM((2, 3, ROWS, HALF), F32),
    ] + [pltpu.VMEM((2, 3, PIECE, HALF), BF16)] * 6 + [
        pltpu.VMEM((2, 2, PIECE, HALF), F32),
        pltpu.VMEM((2, 3, 2, NX, PIECE, HALF), BF16),
        pltpu.VMEM((3, 2 * ROWS, HID), BF16),
        pltpu.VMEM((2, NY, 2, PIECE, WIDE), BF16),
        pltpu.VMEM((2, NY, 2, PIECE, WIDE), BF16),
        pltpu.VMEM((2, 2, 8 * FOLD, ROWS), BF16),
        pltpu.VMEM((2, NZ * FOLD, WIDE), F32),
        pltpu.VMEM((2, 2, 8, FOLD, WIDE), BF16),
        pltpu.VMEM((2, 2, 8, FOLD, WIDE), BF16),
        pltpu.VMEM((3, WIDE, HID), BF16),
        dma((3, 2, 8)), dma((3, 2, 8)),
        dma((3,)), dma((3,)),
        dma((2, 3, 2)), dma((2, 3, 2)),
        dma((2, 3)), dma((2, 3)),
        dma((2, 3, 3)), dma((2, 3, 3)),
        dma((2, 3, 7)), dma((2, 3, 7)),
        dma((2, 3, 2)), dma((2, 3, 2)),
        dma((2, 2, 8)), dma((2, 2, 8)),
        dma((2,)), dma((3,)), dma((3,)),
    ]
    fold = jax.ShapeDtypeStruct((FOLD, WIDE), BF16)
    weight = jax.ShapeDtypeStruct((1, WIDE, HID), BF16)
    hbm5 = (hbm,) * 5
    results = pl.pallas_call(
        body,
        out_shape=(fold, fold, weight, weight, weight),
        in_specs=[vmem, vmem, hbm, hbm, hbm, hbm, hbm],
        out_specs=(vmem, vmem, hbm, hbm, hbm),
        scratch_shapes=scratch,
        compiler_params=pltpu.CompilerParams(
            collective_id=0, has_side_effects=True, vmem_limit_bytes=56 * 1024 * 1024
        ),
    )(
        expert_ids.T, gate_codes.T, tokens, out_grad, gate_weight, up_weight, down_weight
    )
    return pl.pallas_call(
        keep_body,
        out_shape=(fold, fold, weight, weight, weight),
        in_specs=hbm5,
        out_specs=hbm5,
        scratch_shapes=[pltpu.VMEM(out.shape, BF16) for out in (fold, fold, weight, weight, weight)]
        + [dma((2, 8))],
    )(*results)


def solution(mesh):
    placed = (
        P("ctx", ("dp", "tp")),
        P(("ctx", "tp"), None),
        P(("ctx", "tp"), None),
        P(("ctx", "tp"), "dp", None),
        P(("ctx", "tp"), "dp", None),
        P(("ctx", "tp"), "dp", None),
        P("ctx", ("dp", "tp")),
    )
    return jax.shard_map(
        shards,
        mesh=mesh,
        in_specs=placed,
        out_specs=(
            P(("ctx", "tp"), "dp"),
            P(("ctx", "tp"), "dp"),
            P(("ctx", "tp"), "dp", None),
            P(("ctx", "tp"), "dp", None),
            P(("ctx", "tp"), "dp", None),
        ),
        check_vma=False,
    )
```
